32 devices in a mesh: section: 4 (over x, core), fsdp: 8 (over z, y).
Axes of the slice: x: 2, y: 2, z: 4, core: 2. Of those that a mesh axis runs over, the one named last changes fastest.
Arguments:
- student_w: bfloat16 [4, 1, 3072, 3072], P('section', None, 'fsdp'), may hold values from -0.109375 to 0.109375
- teacher_w: float32 [4, 1, 3072, 3072], P('section', None, 'fsdp'), may hold values from -0.109375 to 0.109375
- saved_in: bfloat16 [4, 1, 4, 256, 3072], P('section', None, None, 'fsdp'), may hold values from -6 to 6
- saved_pre: bfloat16 [4, 1, 4, 256, 3072], P('section', None, None, 'fsdp'), may hold values from -6 to 6
- cotangent: bfloat16 [4, 256, 3072], P(None, 'fsdp'), may hold values from -6 to 6
- slot_order: int32 [4], replicated, may hold values from 0 to 3, each once
- layer_counts: int32 [4], replicated, may hold values from 0 to 1, as said below
- teacher_in: bfloat16 [2, 256, 3072], P(None, 'fsdp'), may hold values from -6 to 6
Outputs:
- input_grad: bfloat16 [4, 4, 256, 3072], P('section', None, 'fsdp')
- grad_shards: bfloat16 [4, 1, 3072, 3072], P('section', None, 'fsdp')
- teacher_new: float32 [4, 1, 3072, 3072], P('section', None, 'fsdp')
- teacher_out: bfloat16 [4, 2, 256, 3072], P('section', None, 'fsdp')
The draws below stay inside these ranges and needn't reach their ends.
Inputs may be any that keep to these rules, and one draw needn't show every extreme that they name: `layer_counts`: every section holds 0 to 1 layers; some section holds 1 and some holds none. `slot_order`: each micro-batch appears in exactly one slot.
All inputs are finite; a program needn't handle non-finite values.
Results may differ from the reference program's by a relative error of at most 0.019.
Values may be sent and summed in bfloat16 or wider, within the bound.
No kernel may reach another device: no remote copies, remote signals or barrier semaphores. Data moves between devices by JAX's collectives and lax.ppermute only.
A program may use at most 192 MiB of HBM per device.

```python
import math
import jax
import jax.numpy as jnp
from jax import lax

C = 3072
R = 3072
LAYERS = 1
MB = 4
MB_F = 2
TOK = 32
SECTIONS = 4
TOKENS = 256
N_FSDP = 8


def draw_layer_counts(key, part):
    counts = jax.random.randint(key, (SECTIONS,), 0, LAYERS + 1)
    where_high = jax.random.randint(jax.random.fold_in(key, 7), (), 0, SECTIONS)
    counts = counts.at[where_high].set(LAYERS)
    counts = counts.at[(where_high + 1) % SECTIONS].set(0)
    return counts.astype(jnp.int32)


def with_spikes(values, stream_key, source, target, shards_of, factor):
    def block_of(axis_at):
        return (jnp.arange(values.shape[axis_at]) // (values.shape[axis_at] // shards_of)).reshape((-1,) + (1,) * (values.ndim - 1 - axis_at))

    near = jax.random.permutation(stream_key, shards_of)[block_of(target)]
    other_side = (block_of(target) + shards_of // 2) % shards_of
    return jnp.where((block_of(source) == near) | (block_of(source) == other_side), factor * values, values)


def level_of(stream_key, dims, cuts, smallest, largest):
    loudness = 1.0
    for position, blocks in cuts:
        draws = jax.random.uniform(jax.random.fold_in(jax.random.fold_in(stream_key, 6), position), (blocks,), jnp.float32, smallest / len(cuts), largest / len(cuts))
        loudness = loudness * jnp.repeat(jnp.exp(draws), dims[position] // blocks).reshape((-1,) + (1,) * (len(dims) - 1 - position))
    return loudness


def noise(stream_key, shape, spread, limit, split=(), dtype=jnp.bfloat16):
    array = jax.random.normal(stream_key, shape, jnp.float32) * spread
    if len(split) > 0:
        array = level_of(stream_key, shape, split, -0.22, 0.18) * array
    return jnp.clip(array, min=-limit, max=limit).astype(dtype)


def gaussian_with(rng, extent, scale, most, split, heavy, kind=jnp.bfloat16):
    drawn = scale * jax.random.normal(rng, extent, jnp.float32)
    if split:
        drawn = drawn * level_of(rng, extent, split, -0.22, 0.18)
    return jnp.clip(with_spikes(drawn, jax.random.fold_in(rng, 3), *heavy), -most, most).astype(kind)


def setup_inputs(seed: int = 0) -> dict:
    keys = jax.random.split(jax.random.key(seed), 9)
    return {
        "student_w": noise(keys[0], (SECTIONS, LAYERS, C, R), C ** -0.5, 0.109375, ((0, 4), (2, 8))),
        "teacher_w": noise(keys[1], (SECTIONS, LAYERS, C, R), C ** -0.5, 0.109375, ((0, 4), (2, 8)), jnp.float32),
        "saved_in": gaussian_with(keys[2], (SECTIONS, LAYERS, MB, TOKENS, C), 1.0, 6.0, ((0, 4), (3, 8)), (3, 4, 8, 2.0)),
        "saved_pre": noise(keys[3], (SECTIONS, LAYERS, MB, TOKENS, R), 1.0, 6.0, ((0, 4), (3, 8))),
        "cotangent": noise(keys[4], (MB, TOKENS, C), 1.0, 6.0, ((1, 8),)),
        "slot_order": jax.random.permutation(keys[5], MB).astype(jnp.int32),
        "layer_counts": draw_layer_counts(jax.random.fold_in(keys[8], 71), 0),
        "teacher_in": noise(keys[7], (MB_F, TOKENS, C), 1.0, 6.0, ((1, 8),)),
    }


epsilon = 1e-06
momentum = 0.996

def normalize(values):
    wide = values.astype(jnp.float32)
    factor = lax.rsqrt(lax.optimization_barrier(jnp.mean(wide * wide, axis=-1, keepdims=True)) + epsilon)
    return (wide * factor, factor)

def gelu_slope(pre):
    wide = pre.astype(jnp.float32)
    return 0.5 * (1.0 + jax.scipy.special.erf(wide / math.sqrt(2.0))) + wide * jnp.exp(-0.5 * wide * wide) / math.sqrt(2.0 * math.pi)

def block_terms(normed_low, slopes, scale):
    parts_n = normed_low.reshape(MB, N_FSDP, TOK, C).transpose(1, 0, 2, 3)
    parts_d = slopes.reshape(MB, N_FSDP, TOK, R).transpose(1, 0, 2, 3)

    def add_block(total, pair):
        term = jnp.einsum('kti,ktr->ir', pair[0].astype(jnp.float32), pair[1].astype(jnp.float32)) * scale
        term = lax.optimization_barrier(term.astype(jnp.bfloat16)).astype(jnp.float32)
        return (total + term, None)
    total, _ = lax.scan(add_block, jnp.zeros((C, R), jnp.float32), (parts_n, parts_d))
    return total.astype(jnp.bfloat16)

def reference(student_w, teacher_w, saved_in, saved_pre, cotangent, slot_order, layer_counts, teacher_in):
    scale = 1.0 / math.sqrt(MB * TOKENS)
    grads_by_section = [None] * SECTIONS
    inputs_by_section = [None] * SECTIONS
    upper = cotangent[slot_order]
    for section in reversed(range(SECTIONS)):
        count = layer_counts[section]
        current = upper
        section_grads = [None] * LAYERS
        for layer in reversed(range(LAYERS)):
            active = layer < count
            slopes = (current.astype(jnp.float32) * gelu_slope(saved_pre[section, layer])).astype(jnp.bfloat16)
            slopes = jnp.where(active, slopes, jnp.zeros_like(slopes))
            back = jnp.einsum('ktr,cr->ktc', slopes.astype(jnp.float32), student_w[section, layer].astype(jnp.float32))
            normed, factor = normalize(saved_in[section, layer])
            outgoing = current.astype(jnp.float32) + factor * (back - normed * lax.optimization_barrier(jnp.mean(back * normed, axis=-1, keepdims=True)))
            current = jnp.where(active, outgoing.astype(jnp.bfloat16), current)
            section_grads[layer] = block_terms(normed.astype(jnp.bfloat16), slopes, scale)
        grads_by_section[section] = jnp.stack(section_grads)
        inputs_by_section[section] = current
        upper = current
    grad_shards = jnp.stack(grads_by_section)
    input_grad = jnp.stack(inputs_by_section)
    teacher_new = momentum * teacher_w.astype(jnp.float32) + (1.0 - momentum) * student_w.astype(jnp.float32)
    teacher_low = teacher_new.astype(jnp.bfloat16)
    hidden = teacher_in
    outputs = []
    for section in range(SECTIONS):
        count = layer_counts[section]
        for layer in range(LAYERS):
            normed, _ = normalize(hidden)
            pre = jnp.einsum('ktc,cr->ktr', normed.astype(jnp.bfloat16).astype(jnp.float32), teacher_low[section, layer].astype(jnp.float32))
            result = (hidden.astype(jnp.float32) + jax.nn.gelu(pre, approximate=False)).astype(jnp.bfloat16)
            hidden = jnp.where(layer < count, result, hidden)
        outputs.append(hidden)
    teacher_out = jnp.stack(outputs)
    return (input_grad, grad_shards, teacher_new, teacher_out)
```

```python
import math

import jax
import jax.numpy as jnp
from jax import lax
from jax.sharding import PartitionSpec as P

epsilon = 1e-06
momentum = 0.996
f32 = jnp.float32
bf16 = jnp.bfloat16


def swap(block, axis, bits):
    size = lax.axis_size(axis)
    return lax.ppermute(block, axis, [(i, i ^ bits) for i in range(size)])


def reorder(blocks, axis):
    me = lax.axis_index(axis)
    return jnp.stack(
        [lax.dynamic_index_in_dim(blocks, me ^ j, 0, False) for j in range(blocks.shape[0])]
    )


def gather(block, axis):
    size = lax.axis_size(axis)
    if axis == "section" and size == 4:
        core = swap(block, axis, 1)
        across = swap(block, axis, 2)
        return jnp.stack([block, core, across, swap(across, axis, 1)])
    if axis == "fsdp" and size == 8:
        line = [block] + [swap(block, axis, bits) for bits in (2, 4, 6)]
        other = [swap(b, axis, 1) for b in line]
        return jnp.stack([b for pair in zip(line, other) for b in pair])
    return reorder(lax.all_gather(block, axis, axis=0), axis)


def exchange(blocks, axis):
    return lax.all_to_all(blocks, axis, split_axis=0, concat_axis=0, tiled=True)


def exchange_near(blocks, axis):
    if lax.axis_size(axis) == 4:
        return jnp.stack([blocks[0]] + [swap(blocks[k], axis, k) for k in range(1, 4)])
    return reorder(exchange(reorder(blocks, axis), axis), axis)


def add(a, b):
    return a.astype(f32) + b.astype(f32)


def reduce_near(blocks, axis):
    size = lax.axis_size(axis)
    if axis == "section" and size == 4:
        pairs = blocks.reshape((2, 2) + blocks.shape[1:])
        near = add(pairs[:, 0], swap(pairs[:, 1], axis, 1)).astype(bf16)
        return add(near[0], swap(near[1], axis, 2))
    if axis == "fsdp" and size == 8:
        pairs = blocks.reshape((4, 2) + blocks.shape[1:])
        near = add(pairs[:, 0], swap(pairs[:, 1], axis, 1)).astype(bf16)
        total = near[0].astype(f32)
        for k in (1, 2, 3):
            total = total + swap(near[k], axis, 2 * k).astype(f32)
        return total
    return jnp.sum(exchange_near(blocks, axis).astype(f32), axis=0)


def scatter_from(root, block_at):
    size = lax.axis_size("section")
    me = lax.axis_index("section")
    if size == 4:
        mine = jnp.stack([block_at(me), block_at(me ^ 2)])
        theirs = jnp.stack([block_at(me ^ 1), block_at(me ^ 3)])
        held = jnp.where((me ^ root) & 1 == 0, mine, swap(theirs, "section", 1))
        return jnp.where((me ^ root) & 2 == 0, held[0], swap(held[1], "section", 2))
    blocks = exchange(jnp.stack([block_at(j) for j in range(size)]), "section")
    return lax.dynamic_index_in_dim(blocks, root, 0, False)


def normalize(values):
    wide = values.astype(f32)
    factor = lax.rsqrt(jnp.mean(wide * wide, axis=-1, keepdims=True) + epsilon)
    return (wide * factor, factor)


def gelu_slope(pre):
    wide = pre.astype(f32)
    return 0.5 * (1.0 + jax.scipy.special.erf(wide / math.sqrt(2.0))) + wide * jnp.exp(
        -0.5 * wide * wide
    ) / math.sqrt(2.0 * math.pi)


def times_slope(incoming, pre):
    return (incoming.astype(f32) * gelu_slope(pre)).astype(bf16)


def on_device(
    student_w, teacher_w, saved_in, saved_pre, cotangent, slot_order, layer_counts, teacher_in
):
    sections = lax.axis_size("section")
    groups = lax.axis_size("fsdp")
    section_id = lax.axis_index("section")
    slots, tokens, width = cotangent.shape
    student = student_w[0, 0]
    deep, wide = student.shape
    columns = wide // sections
    rows = slots * tokens
    part = rows // sections
    rows_f = teacher_in.shape[0] * tokens
    part_f = rows_f // sections
    inputs_own = saved_in[0, 0].reshape(rows, width)
    pre_own = saved_pre[0, 0].reshape(rows, wide)
    scale = 1.0 / math.sqrt(rows * groups)

    active = layer_counts > 0
    flags = active.astype(jnp.int32)
    total = jnp.sum(flags)
    up_to = jnp.cumsum(flags)
    ids = jnp.arange(sections)

    def met(place):
        back = jnp.sum(jnp.where(active & (total - up_to == place), ids, 0))
        ahead = jnp.sum(jnp.where(active & (up_to - 1 == place), ids, 0))
        return back, ahead

    done_back = jnp.sum(jnp.where(ids >= section_id, flags, 0))
    done_ahead = jnp.sum(jnp.where(ids <= section_id, flags, 0))

    teacher_new = momentum * teacher_w[0, 0] + (1.0 - momentum) * student.astype(f32)
    teacher_low = teacher_new.astype(bf16)

    def column_block(array):
        return lambda j: lax.dynamic_slice_in_dim(array, j * columns, columns, 1)

    def row_block(array, count):
        return lambda j: lax.dynamic_slice_in_dim(array, j * count, count, 0)

    def to_features(values):
        blocks = values.reshape(values.shape[0], groups, deep).transpose(1, 0, 2)
        return reorder(exchange(blocks, "fsdp"), "fsdp")

    def stage(place, grad, hidden, slopes):
        back, ahead = met(place)
        normed_h, _ = normalize(hidden)
        feats_h = gather(to_features(normed_h.astype(bf16)), "section")
        teacher = scatter_from(ahead, column_block(teacher_low))
        pre = jnp.dot(
            feats_h.reshape(-1, deep), teacher, preferred_element_type=f32
        ).astype(bf16)
        pre = pre.reshape(sections, groups, part_f, columns).transpose(1, 0, 2, 3)
        pre = reduce_near(pre, "fsdp").astype(bf16)
        pre = reorder(exchange_near(pre, "section"), "section")
        pre = pre.transpose(1, 0, 2).reshape(part_f, wide).astype(f32)
        hidden = (hidden.astype(f32) + jax.nn.gelu(pre, approximate=False)).astype(bf16)
        inputs = scatter_from(back, row_block(inputs_own, part))
        weight = scatter_from(back, column_block(student))
        slopes = gather(slopes, "fsdp").reshape(-1, columns)
        dn = lax.dot_general(
            slopes, weight, (((1,), (1,)), ((), ())), preferred_element_type=f32
        ).astype(bf16)
        dn = dn.reshape(groups, sections, part, deep).transpose(1, 0, 2, 3)
        dn = reduce_near(dn, "section").astype(bf16)
        dn = exchange(reorder(dn, "fsdp"), "fsdp")
        dn = dn.transpose(1, 0, 2).reshape(part, width).astype(f32)
        normed, factor = normalize(inputs)
        grad = (
            grad.astype(f32)
            + factor * (dn - normed * jnp.mean(dn * normed, axis=-1, keepdims=True))
        ).astype(bf16)
        feats = gather(to_features(normed.astype(bf16)), "section").transpose(1, 0, 2, 3)
        term = lax.dot_general(
            feats.reshape(-1, deep), slopes, (((0,), (0,)), ((), ())), preferred_element_type=f32
        )
        term = reorder(gather((scale * term).astype(bf16), "section"), "section")
        return grad, hidden, term.transpose(1, 0, 2).reshape(deep, wide), back

    def publish(grad, hidden):
        both = reorder(gather(jnp.concatenate([grad, hidden]), "section"), "section")
        return both[:, :part].reshape(rows, width), both[:, part:].reshape(rows_f, width)

    cot = jnp.stack([cotangent[slot_order[k]] for k in range(slots)]).reshape(rows, width)
    fed = teacher_in.reshape(rows_f, width)
    grad = row_block(cot, part)(section_id)
    hidden = row_block(fed, part_f)(section_id)
    slopes = scatter_from(met(0)[0], column_block(times_slope(cot, pre_own)))
    slopes = reorder(slopes.reshape(sections, part, columns), "section")
    grad, hidden, term, back = stage(0, grad, hidden, slopes)
    weight_grad = jnp.where(section_id == back, term, jnp.zeros_like(term))

    def next_stage(place, operands):
        grad, hidden, out_grad, out_hidden, weight_grad = operands
        seen_grad, seen_hidden = publish(grad, hidden)
        out_grad = jnp.where(done_back == place, seen_grad, out_grad)
        out_hidden = jnp.where(done_ahead == place, seen_hidden, out_hidden)
        pre = scatter_from(met(place)[0], row_block(pre_own, part))
        slopes = times_slope(grad, pre).reshape(part, sections, columns).transpose(1, 0, 2)
        slopes = exchange_near(reorder(slopes, "section"), "section")
        grad, hidden, term, back = stage(place, grad, hidden, slopes)
        weight_grad = jnp.where(section_id == back, term, weight_grad)
        return grad, hidden, out_grad, out_hidden, weight_grad

    carry = (grad, hidden, cot, fed, weight_grad)
    for place in range(1, sections - 1):
        carry = lax.cond(
            place < total, lambda c, place=place: next_stage(place, c), lambda c: c, carry
        )
    grad, hidden, out_grad, out_hidden, weight_grad = carry
    seen_grad, seen_hidden = publish(grad, hidden)
    out_grad = jnp.where(done_back == total, seen_grad, out_grad)
    out_hidden = jnp.where(done_ahead == total, seen_hidden, out_hidden)
    return (
        out_grad.reshape((1,) + cotangent.shape),
        weight_grad[None, None],
        teacher_new[None, None],
        out_hidden.reshape((1,) + teacher_in.shape),
    )


def solution(mesh):
    in_specs = (
        P("section", None, "fsdp", None),
        P("section", None, "fsdp", None),
        P("section", None, None, "fsdp", None),
        P("section", None, None, "fsdp", None),
        P(None, "fsdp", None),
        P(),
        P(),
        P(None, "fsdp", None),
    )
    out_specs = (
        P("section", None, "fsdp", None),
        P("section", None, "fsdp", None),
        P("section", None, "fsdp", None),
        P("section", None, "fsdp", None),
    )
    return jax.shard_map(
        on_device, mesh=mesh, in_specs=in_specs, out_specs=out_specs, check_vma=False
    )
```

```python
import functools
import math

import jax
import jax.numpy as jnp
from jax import lax
from jax.experimental import pallas as pl
from jax.experimental.pallas import tpu as pltpu
from jax.sharding import PartitionSpec as P

epsilon = 1e-06
momentum = 0.996
f32 = jnp.float32
bf16 = jnp.bfloat16

vmem = pl.BlockSpec(memory_space=pltpu.VMEM)
smem = pl.BlockSpec(memory_space=pltpu.SMEM)
anywhere = pl.BlockSpec(memory_space=pl.ANY)
params = pltpu.CompilerParams(vmem_limit_bytes=40 * 2**20)


def swap(block, axis, bits):
    size = lax.axis_size(axis)
    return lax.ppermute(block, axis, [(i, i ^ bits) for i in range(size)])


def reorder(blocks, axis):
    me = lax.axis_index(axis)
    return jnp.stack(
        [lax.dynamic_index_in_dim(blocks, me ^ j, 0, False) for j in range(blocks.shape[0])]
    )


def gather(block, axis):
    size = lax.axis_size(axis)
    if axis == "section" and size == 4:
        core = swap(block, axis, 1)
        across = swap(block, axis, 2)
        return jnp.stack([block, core, across, swap(across, axis, 1)])
    if axis == "fsdp" and size == 8:
        line = [block] + [swap(block, axis, bits) for bits in (2, 4, 6)]
        other = [swap(b, axis, 1) for b in line]
        return jnp.stack([b for pair in zip(line, other) for b in pair])
    return reorder(lax.all_gather(block, axis, axis=0), axis)


def exchange(blocks, axis):
    return lax.all_to_all(blocks, axis, split_axis=0, concat_axis=0, tiled=True)


def exchange_near(blocks, axis):
    if lax.axis_size(axis) == 4:
        return jnp.stack([blocks[0]] + [swap(blocks[k], axis, k) for k in range(1, 4)])
    return reorder(exchange(reorder(blocks, axis), axis), axis)


def add(a, b):
    return a.astype(f32) + b.astype(f32)


def halved(axis, size):
    return (axis, size) in (("section", 4), ("fsdp", 8))


def seat(distance, axis, size):
    if halved(axis, size):
        return (distance & 1) * (size // 2) + (distance >> 1)
    return distance


def reduce_near(blocks, axis):
    size = lax.axis_size(axis)
    if halved(axis, size):
        half = size // 2
        near = add(blocks[:half], swap(blocks[half:], axis, 1)).astype(bf16)
        total = near[0].astype(f32)
        for k in range(1, half):
            total = total + swap(near[k], axis, 2 * k).astype(f32)
        return total
    return jnp.sum(exchange_near(blocks, axis).astype(f32), axis=0)


class Spread:
    def __init__(self, blocks):
        self.size = lax.axis_size("section")
        self.me = lax.axis_index("section")
        if self.size == 4:
            self.mine = blocks[:2]
            self.theirs = swap(blocks[2:], "section", 1)
        else:
            self.all = exchange_near(blocks, "section")

    def take(self, root):
        far = self.me ^ root
        if self.size == 4:
            same = (far & 1) == 0
            across = swap(jnp.where(same, self.mine[1], self.theirs[1]), "section", 2)
            return jnp.where(
                (far & 2) == 0, jnp.where(same, self.mine[0], self.theirs[0]), across
            )
        return lax.dynamic_index_in_dim(self.all, far, 0, False)


def normalize(values):
    wide = values.astype(f32)
    factor = lax.rsqrt(jnp.mean(wide * wide, axis=-1, keepdims=True) + epsilon)
    return (wide * factor, factor)


def gelu_slope(pre):
    wide = pre.astype(f32)
    return 0.5 * (1.0 + lax.erf(wide / math.sqrt(2.0))) + wide * jnp.exp(
        -0.5 * wide * wide
    ) / math.sqrt(2.0 * math.pi)


def times_slope(incoming, pre):
    return (incoming.astype(f32) * gelu_slope(pre)).astype(bf16)


def gelu(pre):
    return 0.5 * pre * (1.0 + lax.erf(pre / math.sqrt(2.0)))


def weights_kernel(sections, me_ref, student_ref, teacher_ref, new_ref, student_out, low_out):
    student = student_ref[...]
    new = momentum * teacher_ref[...] + (1.0 - momentum) * student.astype(f32)
    new_ref[...] = new
    low = new.astype(bf16)
    columns = student.shape[1] // sections
    for j in range(sections):
        place = seat(me_ref[0] ^ j, "section", sections)
        student_out[pl.ds(place, 1)] = student[None, :, j * columns : (j + 1) * columns]
        low_out[pl.ds(place, 1)] = low[None, :, j * columns : (j + 1) * columns]


def split_weights(me, student, teacher, sections):
    deep, wide = student.shape
    tile = next(t for t in (128, 96, 64, 32, 16, deep) if deep % t == 0)
    columns = wide // sections
    whole = pl.BlockSpec((tile, wide), lambda i: (i, 0))
    blocks = pl.BlockSpec((sections, tile, columns), lambda i: (0, i, 0))
    out = jax.ShapeDtypeStruct((sections, deep, columns), bf16)
    return pl.pallas_call(
        functools.partial(weights_kernel, sections),
        grid=(deep // tile,),
        in_specs=[smem, whole, whole],
        out_specs=[whole, blocks, blocks],
        out_shape=[jax.ShapeDtypeStruct(teacher.shape, f32), out, out],
        compiler_params=params,
        name="split_weights",
    )(me, student, teacher)


def back_kernel(me_ref, slopes_ref, weight_ref, out_ref):
    groups, sections, part, columns = slopes_ref.shape
    deep = weight_ref.shape[0]
    weight = weight_ref[...]
    for k in range(groups):
        dn = lax.dot_general(
            slopes_ref[k].reshape(sections * part, columns),
            weight,
            (((1,), (1,)), ((), ())),
            preferred_element_type=f32,
        ).astype(bf16)
        dn = dn.reshape(sections, part, deep)
        for s in range(sections):
            out_ref[seat(s, "section", sections), pl.ds(me_ref[0] ^ k, 1)] = dn[s][None]


def back_product(me, slopes, weight):
    groups, sections, part, _ = slopes.shape
    return pl.pallas_call(
        back_kernel,
        in_specs=[smem, vmem, vmem],
        out_specs=vmem,
        out_shape=jax.ShapeDtypeStruct((sections, groups, part, weight.shape[0]), bf16),
        compiler_params=params,
        name="back_product",
    )(me, slopes, weight)


def grad_kernel(part, scale, me_ref, feats_ref, slopes_ref, out_ref, total_ref):
    groups, sections, _, columns = slopes_ref.shape
    deep = feats_ref.shape[3]
    for k in range(groups):
        feats = feats_ref[:, pl.ds(me_ref[0] ^ k, 1), :part, :]
        term = lax.dot_general(
            feats.reshape(sections * part, deep),
            slopes_ref[k].reshape(sections * part, columns),
            (((0,), (0,)), ((), ())),
            preferred_element_type=f32,
        )
        if k == 0:
            total_ref[...] = term
        else:
            total_ref[...] += term
    out_ref[...] = (scale * total_ref[...]).astype(bf16)


def grad_product(me, feats, slopes, scale):
    _, _, part, columns = slopes.shape
    deep = feats.shape[3]
    return pl.pallas_call(
        functools.partial(grad_kernel, part, scale),
        in_specs=[smem, vmem, vmem],
        out_specs=vmem,
        out_shape=jax.ShapeDtypeStruct((deep, columns), bf16),
        scratch_shapes=[pltpu.VMEM((deep, columns), f32)],
        compiler_params=params,
        name="grad_product",
    )(me, feats, slopes)


def ahead_kernel(part, me_ref, feats_ref, weight_ref, out_ref):
    sections, groups, rows, deep = feats_ref.shape
    part_f = rows - part
    columns = weight_ref.shape[1]
    weight = weight_ref[...]
    for s in range(sections):
        pre = jnp.dot(
            feats_ref[s, :, part:, :].reshape(groups * part_f, deep),
            weight,
            preferred_element_type=f32,
        ).astype(bf16)
        pre = pre.reshape(groups, part_f, columns)
        for j in range(groups):
            out_ref[pl.ds(seat(me_ref[0] ^ j, "fsdp", groups), 1), s] = pre[j][None]


def ahead_product(me, feats, weight, part):
    sections, groups, rows, _ = feats.shape
    return pl.pallas_call(
        functools.partial(ahead_kernel, part),
        in_specs=[smem, vmem, vmem],
        out_specs=vmem,
        out_shape=jax.ShapeDtypeStruct(
            (groups, sections, rows - part, weight.shape[1]), bf16
        ),
        compiler_params=params,
        name="ahead_product",
    )(me, feats, weight)


def slopes_kernel(me_ref, grad_ref, pre_ref, out_ref):
    slopes = times_slope(grad_ref[...], pre_ref[...])
    sections, _, columns = out_ref.shape
    for j in range(sections):
        out_ref[pl.ds(me_ref[0] ^ j, 1)] = slopes[None, :, j * columns : (j + 1) * columns]


def slope_blocks(me, grad, pre, sections):
    part, wide = pre.shape
    return pl.pallas_call(
        slopes_kernel,
        in_specs=[smem, vmem, vmem],
        out_specs=vmem,
        out_shape=jax.ShapeDtypeStruct((sections, part, wide // sections), bf16),
        compiler_params=params,
        name="slope_blocks",
    )(me, grad, pre)


def update_kernel(grad_ref, inputs_ref, dn_ref, out_ref):
    groups, _, deep = dn_ref.shape
    dn = jnp.concatenate([dn_ref[j].astype(f32) for j in range(groups)], axis=1)
    normed, factor = normalize(inputs_ref[...])
    grad = grad_ref[...].astype(f32) + factor * (
        dn - normed * jnp.mean(dn * normed, axis=-1, keepdims=True)
    )
    out_ref[...] = grad.astype(bf16)


def update(grad, inputs, dn):
    return pl.pallas_call(
        update_kernel,
        in_specs=[vmem, vmem, vmem],
        out_specs=vmem,
        out_shape=jax.ShapeDtypeStruct(grad.shape, bf16),
        compiler_params=params,
        name="update",
    )(grad, inputs, dn)


def feature_blocks(inputs, hidden, groups):
    both = jnp.concatenate([normalize(inputs)[0], normalize(hidden)[0]]).astype(bf16)
    return both.reshape(both.shape[0], groups, -1).transpose(1, 0, 2)


def store_kernel(own_ref, term_ref, old_ref, out_ref, sem):
    sections, _, columns = term_ref.shape

    @pl.when(own_ref[0] == 1)
    def _():
        copies = [
            pltpu.make_async_copy(
                term_ref.at[j], out_ref.at[:, pl.ds(j * columns, columns)], sem.at[j]
            )
            for j in range(sections)
        ]
        for copy in copies:
            copy.start()
        for copy in copies:
            copy.wait()


def store(own, term, old):
    return pl.pallas_call(
        store_kernel,
        in_specs=[smem, anywhere, anywhere],
        out_specs=anywhere,
        out_shape=jax.ShapeDtypeStruct(old.shape, bf16),
        scratch_shapes=[pltpu.SemaphoreType.DMA((term.shape[0],))],
        input_output_aliases={2: 0},
        compiler_params=params,
        name="store",
    )(own, term, old)


def on_device(
    student_w, teacher_w, saved_in, saved_pre, cotangent, slot_order, layer_counts, teacher_in
):
    sections = lax.axis_size("section")
    groups = lax.axis_size("fsdp")
    section_id = lax.axis_index("section")
    group_id = lax.axis_index("fsdp")
    me_s = section_id.astype(jnp.int32)[None]
    me_f = group_id.astype(jnp.int32)[None]
    slots, tokens, width = cotangent.shape
    student = student_w[0, 0]
    deep, wide = student.shape
    columns = wide // sections
    rows = slots * tokens
    part = rows // sections
    rows_f = teacher_in.shape[0] * tokens
    part_f = rows_f // sections
    aligned = part % 16 == 0 and part_f % 16 == 0 and deep % 128 == 0 and columns % 128 == 0
    inputs_own = saved_in[0, 0].reshape(rows, width)
    pre_own = saved_pre[0, 0].reshape(rows, wide)
    scale = 1.0 / math.sqrt(rows * groups)

    active = layer_counts > 0
    flags = active.astype(jnp.int32)
    total = jnp.sum(flags)
    up_to = jnp.cumsum(flags)
    done_back = total - up_to + flags
    ids = jnp.arange(sections)

    def met(place):
        back = jnp.sum(jnp.where(active & (total - up_to == place), ids, 0))
        ahead = jnp.sum(jnp.where(active & (up_to - 1 == place), ids, 0))
        return back, ahead

    distances = sorted(range(sections), key=lambda k: seat(k, "section", sections))

    def row_blocks(array, count):
        return jnp.stack(
            [
                lax.dynamic_slice_in_dim(array, (section_id ^ k) * count, count, 0)
                for k in distances
            ]
        )

    def column_blocks(array):
        return jnp.stack(
            [
                lax.dynamic_slice_in_dim(array, (section_id ^ k) * columns, columns, 1)
                for k in distances
            ]
        )

    if aligned:
        teacher_new, student_blocks, low_blocks = split_weights(
            me_s, student, teacher_w[0, 0], sections
        )
    else:
        teacher_new = momentum * teacher_w[0, 0] + (1.0 - momentum) * student.astype(f32)
        student_blocks = column_blocks(student)
        low_blocks = column_blocks(teacher_new.astype(bf16))

    def back_part(slopes, weight):
        if aligned:
            return back_product(me_f, slopes, weight)
        dn = jnp.einsum("gspr,dr->sgpd", slopes, weight, preferred_element_type=f32)
        return reorder(dn.astype(bf16).transpose(1, 0, 2, 3), "fsdp").transpose(1, 0, 2, 3)

    def ahead_part(feats, weight):
        if aligned:
            return ahead_product(me_f, feats, weight, part)
        pre = jnp.einsum("sgpd,dr->gspr", feats[:, :, part:], weight, preferred_element_type=f32)
        return reorder(pre.astype(bf16), "fsdp")

    def grad_part(feats, slopes):
        if aligned:
            return grad_product(me_f, feats, slopes, scale)
        feats = reorder(feats[:, :, :part].transpose(1, 0, 2, 3), "fsdp")
        term = jnp.einsum("gspd,gspr->dr", feats, slopes, preferred_element_type=f32)
        return (scale * term).astype(bf16)

    def slope_part(grad, pre):
        if aligned:
            return slope_blocks(me_s, grad, pre, sections)
        slopes = times_slope(grad, pre).reshape(part, sections, columns).transpose(1, 0, 2)
        return reorder(slopes, "section")

    def update_part(grad, inputs, dn):
        if aligned:
            return update(grad, inputs, dn)
        dn = dn.transpose(1, 0, 2).reshape(part, width).astype(f32)
        normed, factor = normalize(inputs)
        grad = grad.astype(f32) + factor * (
            dn - normed * jnp.mean(dn * normed, axis=-1, keepdims=True)
        )
        return grad.astype(bf16)

    def store_part(own, term, old):
        if aligned:
            return store(own.astype(jnp.int32)[None], term, old)
        return jnp.where(own, term.transpose(1, 0, 2).reshape(deep, wide), old)

    def stage(place, grad, hidden, slopes, inputs, weight_grad, spreads):
        student_spread, low_spread, saved_spread = spreads
        back, ahead = met(place)
        next_back, _ = met(place + 1)
        saved = saved_spread.take(next_back)
        feats = exchange(feature_blocks(inputs, hidden, groups), "fsdp")
        feats = gather(feats, "section")
        low = low_spread.take(ahead)
        weight = student_spread.take(back)
        slopes = gather(slopes, "fsdp")
        pre = reduce_near(ahead_part(feats, low), "fsdp").astype(bf16)
        pre = reorder(exchange_near(pre, "section"), "section")
        pre = pre.transpose(1, 0, 2).reshape(part_f, wide).astype(f32)
        hidden = (hidden.astype(f32) + gelu(pre)).astype(bf16)
        dn = reduce_near(back_part(slopes, weight), "section").astype(bf16)
        dn = exchange(dn, "fsdp")
        grad = update_part(grad, inputs, dn)
        term = lax.all_gather(grad_part(feats, slopes), "section", axis=0)
        weight_grad = store_part(section_id == back, term, weight_grad)
        return grad, hidden, saved, weight_grad

    cot = jnp.stack([cotangent[slot_order[k]] for k in range(slots)]).reshape(rows, width)
    fed = teacher_in.reshape(rows_f, width)
    grad = lax.dynamic_slice_in_dim(cot, section_id * part, part, 0)
    hidden = lax.dynamic_slice_in_dim(fed, section_id * part_f, part_f, 0)
    slopes = Spread(column_blocks(times_slope(cot, pre_own))).take(met(0)[0])
    slopes = reorder(slopes.reshape(sections, part, columns), "section")
    spreads = (
        Spread(student_blocks),
        Spread(low_blocks),
        Spread(
            jnp.concatenate([row_blocks(inputs_own, part), row_blocks(pre_own, part)], axis=1)
        ),
    )
    inputs = spreads[2].take(met(0)[0])[:part]
    weight_grad = jnp.zeros((deep, wide), bf16)
    grads = jnp.zeros((sections,) + grad.shape, bf16).at[0].set(grad)
    hiddens = jnp.zeros((sections,) + hidden.shape, bf16).at[0].set(hidden)
    grad, hidden, saved, weight_grad = stage(
        0, grad, hidden, slopes, inputs, weight_grad, spreads
    )
    grads = grads.at[1].set(grad)
    hiddens = hiddens.at[1].set(hidden)

    def round_of(place, carry):
        grads, hiddens, saved, weight_grad = carry
        grad = lax.dynamic_index_in_dim(grads, place, 0, False)
        hidden = lax.dynamic_index_in_dim(hiddens, place, 0, False)
        slopes = exchange_near(slope_part(grad, saved[part:]), "section")
        grad, hidden, saved, weight_grad = stage(
            place, grad, hidden, slopes, saved[:part], weight_grad, spreads
        )
        grads = lax.dynamic_update_index_in_dim(grads, grad, place + 1, 0)
        hiddens = lax.dynamic_update_index_in_dim(hiddens, hidden, place + 1, 0)
        return grads, hiddens, saved, weight_grad

    grads, hiddens, _, weight_grad = lax.fori_loop(
        1, total, round_of, (grads, hiddens, saved, weight_grad)
    )
    outs = exchange(
        jnp.stack(
            [
                jnp.concatenate(
                    [
                        lax.dynamic_index_in_dim(grads, done_back[s], 0, False),
                        lax.dynamic_index_in_dim(hiddens, up_to[s], 0, False),
                    ]
                )
                for s in range(sections)
            ]
        ),
        "section",
    )
    return (
        outs[:, :part].reshape((1,) + cotangent.shape),
        weight_grad[None, None],
        teacher_new[None, None],
        outs[:, part:].reshape((1,) + teacher_in.shape),
    )


def solution(mesh):
    in_specs = (
        P("section", None, "fsdp", None),
        P("section", None, "fsdp", None),
        P("section", None, None, "fsdp", None),
        P("section", None, None, "fsdp", None),
        P(None, "fsdp", None),
        P(),
        P(),
        P(None, "fsdp", None),
    )
    out_specs = (
        P("section", None, "fsdp", None),
        P("section", None, "fsdp", None),
        P("section", None, "fsdp", None),
        P("section", None, "fsdp", None),
    )
    return jax.shard_map(
        on_device, mesh=mesh, in_specs=in_specs, out_specs=out_specs, check_vma=False
    )
```

```python
import functools
import math

import jax
import jax.numpy as jnp
from jax import lax
from jax.experimental import pallas as pl
from jax.experimental.pallas import tpu as pltpu
from jax.sharding import PartitionSpec as P

epsilon = 1e-06
momentum = 0.996
f32 = jnp.float32
bf16 = jnp.bfloat16


def swap(block, axis, bits):
    size = lax.axis_size(axis)
    return lax.ppermute(block, axis, [(i, i ^ bits) for i in range(size)])


def reorder(blocks, axis):
    me = lax.axis_index(axis)
    return jnp.stack(
        [lax.dynamic_index_in_dim(blocks, me ^ j, 0, False) for j in range(blocks.shape[0])]
    )


def gather(block, axis):
    return reorder(lax.all_gather(block, axis, axis=0), axis)


def exchange(blocks, axis):
    return lax.all_to_all(blocks, axis, split_axis=0, concat_axis=0, tiled=True)


def exchange_near(blocks, axis):
    return reorder(exchange(reorder(blocks, axis), axis), axis)


def add(a, b):
    return a.astype(f32) + b.astype(f32)


def reduce_near(blocks, axis):
    return jnp.sum(exchange_near(blocks, axis).astype(f32), axis=0)


def scatter_from(root, block_at):
    size = lax.axis_size("section")
    blocks = exchange(jnp.stack([block_at(j) for j in range(size)]), "section")
    return lax.dynamic_index_in_dim(blocks, root, 0, False)


def normalize(values):
    wide = values.astype(f32)
    factor = lax.rsqrt(jnp.mean(wide * wide, axis=-1, keepdims=True) + epsilon)
    return (wide * factor, factor)


def gelu_slope(pre):
    wide = pre.astype(f32)
    return 0.5 * (1.0 + lax.erf(wide / math.sqrt(2.0))) + wide * jnp.exp(
        -0.5 * wide * wide
    ) / math.sqrt(2.0 * math.pi)


def times_slope(incoming, pre):
    return (incoming.astype(f32) * gelu_slope(pre)).astype(bf16)


def on_any_mesh(
    student_w, teacher_w, saved_in, saved_pre, cotangent, slot_order, layer_counts, teacher_in
):
    sections = lax.axis_size("section")
    groups = lax.axis_size("fsdp")
    section_id = lax.axis_index("section")
    slots, tokens, width = cotangent.shape
    student = student_w[0, 0]
    deep, wide = student.shape
    columns = wide // sections
    rows = slots * tokens
    part = rows // sections
    rows_f = teacher_in.shape[0] * tokens
    part_f = rows_f // sections
    inputs_own = saved_in[0, 0].reshape(rows, width)
    pre_own = saved_pre[0, 0].reshape(rows, wide)
    scale = 1.0 / math.sqrt(rows * groups)

    active = layer_counts > 0
    flags = active.astype(jnp.int32)
    total = jnp.sum(flags)
    up_to = jnp.cumsum(flags)
    ids = jnp.arange(sections)

    def met(place):
        back = jnp.sum(jnp.where(active & (total - up_to == place), ids, 0))
        ahead = jnp.sum(jnp.where(active & (up_to - 1 == place), ids, 0))
        return back, ahead

    done_back = jnp.sum(jnp.where(ids >= section_id, flags, 0))
    done_ahead = jnp.sum(jnp.where(ids <= section_id, flags, 0))

    teacher_new = momentum * teacher_w[0, 0] + (1.0 - momentum) * student.astype(f32)
    teacher_low = teacher_new.astype(bf16)

    def column_block(array):
        return lambda j: lax.dynamic_slice_in_dim(array, j * columns, columns, 1)

    def row_block(array, count):
        return lambda j: lax.dynamic_slice_in_dim(array, j * count, count, 0)

    def to_features(values):
        blocks = values.reshape(values.shape[0], groups, deep).transpose(1, 0, 2)
        return reorder(exchange(blocks, "fsdp"), "fsdp")

    def stage(place, grad, hidden, slopes):
        back, ahead = met(place)
        normed_h, _ = normalize(hidden)
        feats_h = gather(to_features(normed_h.astype(bf16)), "section")
        teacher = scatter_from(ahead, column_block(teacher_low))
        pre = jnp.dot(
            feats_h.reshape(-1, deep), teacher, preferred_element_type=f32
        ).astype(bf16)
        pre = pre.reshape(sections, groups, part_f, columns).transpose(1, 0, 2, 3)
        pre = reduce_near(pre, "fsdp").astype(bf16)
        pre = reorder(exchange_near(pre, "section"), "section")
        pre = pre.transpose(1, 0, 2).reshape(part_f, wide).astype(f32)
        hidden = (hidden.astype(f32) + jax.nn.gelu(pre, approximate=False)).astype(bf16)
        inputs = scatter_from(back, row_block(inputs_own, part))
        weight = scatter_from(back, column_block(student))
        slopes = gather(slopes, "fsdp").reshape(-1, columns)
        dn = lax.dot_general(
            slopes, weight, (((1,), (1,)), ((), ())), preferred_element_type=f32
        ).astype(bf16)
        dn = dn.reshape(groups, sections, part, deep).transpose(1, 0, 2, 3)
        dn = reduce_near(dn, "section").astype(bf16)
        dn = exchange(reorder(dn, "fsdp"), "fsdp")
        dn = dn.transpose(1, 0, 2).reshape(part, width).astype(f32)
        normed, factor = normalize(inputs)
        grad = (
            grad.astype(f32)
            + factor * (dn - normed * jnp.mean(dn * normed, axis=-1, keepdims=True))
        ).astype(bf16)
        feats = gather(to_features(normed.astype(bf16)), "section").transpose(1, 0, 2, 3)
        term = lax.dot_general(
            feats.reshape(-1, deep), slopes, (((0,), (0,)), ((), ())), preferred_element_type=f32
        )
        term = reorder(gather((scale * term).astype(bf16), "section"), "section")
        return grad, hidden, term.transpose(1, 0, 2).reshape(deep, wide), back

    def publish(grad, hidden):
        both = reorder(gather(jnp.concatenate([grad, hidden]), "section"), "section")
        return both[:, :part].reshape(rows, width), both[:, part:].reshape(rows_f, width)

    cot = jnp.stack([cotangent[slot_order[k]] for k in range(slots)]).reshape(rows, width)
    fed = teacher_in.reshape(rows_f, width)
    grad = row_block(cot, part)(section_id)
    hidden = row_block(fed, part_f)(section_id)
    slopes = scatter_from(met(0)[0], column_block(times_slope(cot, pre_own)))
    slopes = reorder(slopes.reshape(sections, part, columns), "section")
    grad, hidden, term, back = stage(0, grad, hidden, slopes)
    weight_grad = jnp.where(section_id == back, term, jnp.zeros_like(term))

    def next_stage(place, operands):
        grad, hidden, out_grad, out_hidden, weight_grad = operands
        seen_grad, seen_hidden = publish(grad, hidden)
        out_grad = jnp.where(done_back == place, seen_grad, out_grad)
        out_hidden = jnp.where(done_ahead == place, seen_hidden, out_hidden)
        pre = scatter_from(met(place)[0], row_block(pre_own, part))
        slopes = times_slope(grad, pre).reshape(part, sections, columns).transpose(1, 0, 2)
        slopes = exchange_near(reorder(slopes, "section"), "section")
        grad, hidden, term, back = stage(place, grad, hidden, slopes)
        weight_grad = jnp.where(section_id == back, term, weight_grad)
        return grad, hidden, out_grad, out_hidden, weight_grad

    carry = (grad, hidden, cot, fed, weight_grad)
    for place in range(1, sections - 1):
        carry = lax.cond(
            place < total, lambda c, place=place: next_stage(place, c), lambda c: c, carry
        )
    grad, hidden, out_grad, out_hidden, weight_grad = carry
    seen_grad, seen_hidden = publish(grad, hidden)
    out_grad = jnp.where(done_back == total, seen_grad, out_grad)
    out_hidden = jnp.where(done_ahead == total, seen_hidden, out_hidden)
    return (
        out_grad.reshape((1,) + cotangent.shape),
        weight_grad[None, None],
        teacher_new[None, None],
        out_hidden.reshape((1,) + teacher_in.shape),
    )


vmem = pl.BlockSpec(memory_space=pltpu.VMEM)
smem = pl.BlockSpec(memory_space=pltpu.SMEM)
anywhere = pl.BlockSpec(memory_space=pl.ANY)
params = pltpu.CompilerParams(vmem_limit_bytes=40 * 2**20)


def call(body, name, operands, spaces, out_shape, out_spaces, **more):
    return pl.pallas_call(
        body,
        in_specs=spaces,
        out_specs=out_spaces,
        out_shape=out_shape,
        compiler_params=params,
        name=name,
        **more,
    )(*operands)


def shaped(shape, dtype=bf16):
    return jax.ShapeDtypeStruct(shape, dtype)


def window(block, size):
    return pl.ds(pl.multiple_of(block * size, size), size)


class Plan:
    def __init__(self, sections):
        self.section, self.group, self.total, self.back = 0, 1, 2, 3
        self.ahead = self.back + sections + 1
        self.done_back = self.ahead + sections + 1
        self.done_ahead = self.done_back + sections
        self.size = self.done_ahead + sections


def plan_kernel(where, counts_ref, section_ref, group_ref, out_ref):
    sections = counts_ref.shape[0]
    out_ref[where.section] = section_ref[0]
    out_ref[where.group] = group_ref[0]
    seen = jnp.int32(0)
    for s in range(sections):
        out_ref[where.ahead + seen] = jnp.int32(s)
        seen = seen + (counts_ref[s] > 0).astype(jnp.int32)
        out_ref[where.done_ahead + s] = seen
    out_ref[where.total] = seen
    out_ref[where.ahead + sections] = jnp.int32(0)
    seen = jnp.int32(0)
    for s in reversed(range(sections)):
        out_ref[where.back + seen] = jnp.int32(s)
        seen = seen + (counts_ref[s] > 0).astype(jnp.int32)
        out_ref[where.done_back + s] = seen
    out_ref[where.back + sections] = jnp.int32(0)


def make_plan(where, counts):
    me = [lax.axis_index(axis).astype(jnp.int32)[None] for axis in ("section", "fsdp")]
    return call(
        functools.partial(plan_kernel, where),
        "make_plan",
        (counts, *me),
        [smem] * 3,
        shaped((where.size,), jnp.int32),
        smem,
    )


def first_kernel(where, plan, order, cot, pre, near_out, far_out, grad_out):
    sections, _, columns = near_out.shape[1:]
    me = plan[where.section]
    grad_out[...] = cot[order[me]]
    for distance in range(sections):
        target = me ^ distance
        out = (near_out, far_out)[distance & 1]
        for slot in range(sections):
            out[distance >> 1, pl.ds(slot ^ target, 1)] = times_slope(
                cot[order[slot], :, window(target, columns)],
                pre[slot, :, window(target, columns)],
            )[None]


def first_slopes(where, plan, order, cot, pre):
    sections, part, wide = pre.shape
    half = shaped((sections // 2, sections, part, wide // sections))
    return call(
        functools.partial(first_kernel, where),
        "first_slopes",
        (plan, order, cot, pre),
        [smem, smem, vmem, vmem],
        [half, half, shaped((part, wide))],
        [vmem] * 3,
    )


def weights_kernel(where, plan, student_ref, teacher_ref, new_ref, s_near, s_far, t_near, t_far):
    sections, columns = 2 * s_near.shape[0], s_near.shape[2]
    new_ref[...] = momentum * teacher_ref[...] + (1.0 - momentum) * student_ref[...].astype(f32)
    for distance in range(sections):
        cols = window(plan[where.section] ^ distance, columns)
        (s_near, s_far)[distance & 1][distance >> 1] = student_ref[:, cols]
        (t_near, t_far)[distance & 1][distance >> 1] = new_ref[:, cols].astype(bf16)


def split_weights(where, plan, student, teacher, sections):
    deep, wide = student.shape
    tile = 64
    columns = wide // sections
    whole = pl.BlockSpec((tile, wide), lambda i: (i, 0))
    half = pl.BlockSpec((sections // 2, tile, columns), lambda i: (0, i, 0))
    out = shaped((sections // 2, deep, columns))
    return call(
        functools.partial(weights_kernel, where),
        "split_weights",
        (plan, student, teacher),
        [smem, whole, whole],
        [shaped(teacher.shape, f32)] + [out] * 4,
        [whole] + [half] * 4,
        grid=(deep // tile,),
    )


def rows_kernel(where, plan, inputs_ref, pre_ref, near_out, far_out):
    part = inputs_ref.shape[1]
    for distance in range(inputs_ref.shape[0]):
        target = plan[where.section] ^ distance
        out = (near_out, far_out)[distance & 1]
        out[distance >> 1, :part] = inputs_ref[target]
        out[distance >> 1, part:] = pre_ref[target]


def split_rows(where, plan, inputs, pre):
    sections, part, wide = inputs.shape
    half = shaped((sections // 2, 2 * part, wide))
    return call(
        functools.partial(rows_kernel, where),
        "split_rows",
        (plan, inputs, pre),
        [smem, vmem, vmem],
        [half, half],
        [vmem] * 2,
    )


def send_kernel(where, root_at, plan, place, *refs):
    count = len(root_at)
    outs, sem = refs[2 * count : 3 * count], refs[3 * count]
    for i, at in enumerate(root_at):
        distance = plan[where.section] ^ plan[at + place[0]]
        for core in (0, 1):

            @pl.when((distance & 1) == core)
            def _(i=i, core=core):
                pltpu.make_async_copy(refs[2 * i + core].at[1], outs[i], sem.at[i]).start()

    for i in range(count):
        pltpu.make_async_copy(refs[2 * i].at[1], outs[i], sem.at[i]).wait()


def across(where, plan, place, roots, pairs):
    flat = [half for pair in pairs for half in pair]
    sent = call(
        functools.partial(send_kernel, where, tuple(roots)),
        "send_blocks",
        (plan, place, *flat),
        [smem, smem] + [anywhere] * len(flat),
        [shaped(near.shape[1:]) for near, _ in pairs],
        [vmem] * len(pairs),
        scratch_shapes=[pltpu.SemaphoreType.DMA((len(pairs),))],
    )
    return [swap(block, "section", 2) for block in sent]


def fetch(distance, near, far, came, held, sem):
    choices = ((near.at[0], 0), (far.at[0], 1), (came, 2), (came, 3))
    for source, at in choices:

        @pl.when(distance == at)
        def _(source=source):
            pltpu.make_async_copy(source, held, sem).start()

    pltpu.make_async_copy(came, held, sem).wait()


def take_kernel(where, plan, place, near, far, came, inputs_out, pre_out, sem):
    distance = plan[where.section] ^ plan[where.back + place[0]]
    part = inputs_out.shape[0]
    for j, out in enumerate((inputs_out, pre_out)):
        rows = pl.ds(j * part, part)
        for source, at in ((near.at[0], 0), (far.at[0], 1), (came, 2), (came, 3)):

            @pl.when(distance == at)
            def _(source=source, out=out, rows=rows, j=j):
                pltpu.make_async_copy(source.at[rows], out, sem.at[j]).start()

    for j, out in enumerate((inputs_out, pre_out)):
        pltpu.make_async_copy(came.at[pl.ds(j * part, part)], out, sem.at[j]).wait()


def take_rows(where, plan, place, near, far, came):
    part = came.shape[0] // 2
    return call(
        functools.partial(take_kernel, where),
        "take_rows",
        (plan, place, near, far, came),
        [smem, smem] + [anywhere] * 3,
        [shaped((part, came.shape[1]))] * 2,
        [vmem] * 2,
        scratch_shapes=[pltpu.SemaphoreType.DMA((2,))],
    )


def choose_kernel(where, plan, near, far, came, out, sem):
    distance = plan[where.section] ^ plan[where.back]
    fetch(distance, near, far, came, out, sem)


def choose(where, plan, near, far, came):
    return call(
        functools.partial(choose_kernel, where),
        "choose",
        (plan, near, far, came),
        [smem] + [anywhere] * 3,
        shaped(came.shape),
        vmem,
        scratch_shapes=[pltpu.SemaphoreType.DMA],
    )


def features_kernel(inputs_ref, hidden_ref, out_ref):
    groups, _, deep = out_ref.shape
    part = inputs_ref.shape[0]
    for rows, ref in ((pl.ds(0, part), inputs_ref), (pl.ds(part, hidden_ref.shape[0]), hidden_ref)):
        normed = normalize(ref[...])[0].astype(bf16)
        for j in range(groups):
            out_ref[j, rows] = normed[:, j * deep : (j + 1) * deep]


def features(inputs, hidden, groups):
    rows = inputs.shape[0] + hidden.shape[0]
    return call(
        features_kernel,
        "features",
        (inputs, hidden),
        [vmem, vmem],
        shaped((groups, rows, inputs.shape[1] // groups)),
        vmem,
    )


def back_kernel(where, plan, place, slopes_ref, near, far, came, stay_out, go_out, weight, sem):
    groups, sections, part, columns = slopes_ref.shape
    distance = plan[where.section] ^ plan[where.back + place[0]]
    fetch(distance, near, far, came, weight, sem)
    for k in range(groups):
        dn = lax.dot_general(
            slopes_ref[k].reshape(sections * part, columns),
            weight[...],
            (((1,), (1,)), ((), ())),
            preferred_element_type=f32,
        ).astype(bf16)
        dn = dn.reshape(sections, part, weight.shape[0])
        for s in range(sections):
            out = (stay_out, go_out)[s & 1]
            out[s >> 1, pl.ds(plan[where.group] ^ k, 1)] = dn[s][None]


def back_product(where, plan, place, slopes, near, far, came):
    groups, sections, part, _ = slopes.shape
    out = shaped((sections // 2, groups, part, came.shape[0]))
    return call(
        functools.partial(back_kernel, where),
        "back_product",
        (plan, place, slopes, near, far, came),
        [smem, smem, vmem] + [anywhere] * 3,
        [out, out],
        [vmem] * 2,
        scratch_shapes=[pltpu.VMEM(came.shape, bf16), pltpu.SemaphoreType.DMA],
    )


def ahead_kernel(where, part, plan, place, feats_ref, near, far, came, stay_out, go_out, weight, sem):
    sections, groups, rows, deep = feats_ref.shape
    part_f, columns = rows - part, came.shape[1]
    distance = plan[where.section] ^ plan[where.ahead + place[0]]
    fetch(distance, near, far, came, weight, sem)
    side = plan[where.group] & 1
    for s in range(sections):
        pre = jnp.dot(
            feats_ref[s, :, part:, :].reshape(groups * part_f, deep),
            weight[...],
            preferred_element_type=f32,
        ).astype(bf16)
        pre = pre.reshape(groups, part_f, columns)
        for j in range(0, groups, 2):
            seat = (plan[where.group] ^ j) >> 1
            stay_out[pl.ds(seat, 1), s] = jnp.where(side == 0, pre[j], pre[j + 1])[None]
            go_out[pl.ds(seat, 1), s] = jnp.where(side == 0, pre[j + 1], pre[j])[None]


def ahead_product(where, part, plan, place, feats, near, far, came):
    sections, groups, rows, _ = feats.shape
    out = shaped((groups // 2, sections, rows - part, came.shape[1]))
    return call(
        functools.partial(ahead_kernel, where, part),
        "ahead_product",
        (plan, place, feats, near, far, came),
        [smem, smem, vmem] + [anywhere] * 3,
        [out, out],
        [vmem] * 2,
        scratch_shapes=[pltpu.VMEM(came.shape, bf16), pltpu.SemaphoreType.DMA],
    )


def grad_kernel(where, scale, plan, feats_ref, slopes_ref, out_ref, total_ref):
    groups, sections, part, columns = slopes_ref.shape
    deep = feats_ref.shape[3]
    for k in range(groups):
        feats = feats_ref[:, pl.ds(plan[where.group] ^ k, 1), :part, :]
        term = lax.dot_general(
            feats.reshape(sections * part, deep),
            slopes_ref[k].reshape(sections * part, columns),
            (((0,), (0,)), ((), ())),
            preferred_element_type=f32,
        )
        if k == 0:
            total_ref[...] = term
        else:
            total_ref[...] += term
    out_ref[...] = (scale * total_ref[...]).astype(bf16)


def grad_product(where, scale, plan, feats, slopes):
    size = (feats.shape[3], slopes.shape[3])
    return call(
        functools.partial(grad_kernel, where, scale),
        "grad_product",
        (plan, feats, slopes),
        [smem, vmem, vmem],
        shaped(size),
        vmem,
        scratch_shapes=[pltpu.VMEM(size, f32)],
    )


def slopes_kernel(where, plan, grad_ref, pre_ref, out_ref):
    sections, _, columns = out_ref.shape
    for distance in range(sections):
        cols = window(plan[where.section] ^ distance, columns)
        out_ref[distance] = times_slope(grad_ref[:, cols], pre_ref[:, cols])


def slope_blocks(where, plan, grad, pre, sections):
    part, wide = pre.shape
    return call(
        functools.partial(slopes_kernel, where),
        "slope_blocks",
        (plan, grad, pre),
        [smem, vmem, vmem],
        shaped((sections, part, wide // sections)),
        vmem,
    )


def write_seen(done, sections, plan, place, values, outs, sem):
    for start in (True, False):
        for s in range(sections):

            @pl.when(plan[done + s] == place[0] + 1)
            def _(s=s, start=start):
                copy = pltpu.make_async_copy(values, outs.at[s], sem.at[s])
                copy.start() if start else copy.wait()


def update_kernel(where, plan, place, grad_ref, inputs_ref, dn_ref, old, out_ref, outs, sem):
    groups = dn_ref.shape[0]
    dn = jnp.concatenate([dn_ref[j].astype(f32) for j in range(groups)], axis=1)
    normed, factor = normalize(inputs_ref[...])
    grad = grad_ref[...].astype(f32) + factor * (
        dn - normed * jnp.mean(dn * normed, axis=-1, keepdims=True)
    )
    out_ref[...] = grad.astype(bf16)
    write_seen(where.done_back, old.shape[0], plan, place, out_ref, outs, sem)


def update(where, plan, place, grad, inputs, dn, outs):
    return call(
        functools.partial(update_kernel, where),
        "update",
        (plan, place, grad, inputs, dn, outs),
        [smem, smem, vmem, vmem, vmem, anywhere],
        [shaped(grad.shape), shaped(outs.shape)],
        [vmem, anywhere],
        scratch_shapes=[pltpu.SemaphoreType.DMA((outs.shape[0],))],
        input_output_aliases={5: 1},
    )


def hidden_kernel(where, plan, place, hidden_ref, pre_ref, old, out_ref, outs, sem):
    sections, _, columns = pre_ref.shape
    for distance in range(sections):
        cols = window(plan[where.section] ^ distance, columns)
        pre = pre_ref[distance].astype(f32)
        gelu = 0.5 * pre * (1.0 + lax.erf(pre / math.sqrt(2.0)))
        out_ref[:, cols] = (hidden_ref[:, cols].astype(f32) + gelu).astype(bf16)
    write_seen(where.done_ahead, old.shape[0], plan, place, out_ref, outs, sem)


def update_hidden(where, plan, place, hidden, pre, outs):
    return call(
        functools.partial(hidden_kernel, where),
        "update_hidden",
        (plan, place, hidden, pre, outs),
        [smem, smem, vmem, vmem, anywhere],
        [shaped(hidden.shape), shaped(outs.shape)],
        [vmem, anywhere],
        scratch_shapes=[pltpu.SemaphoreType.DMA((outs.shape[0],))],
        input_output_aliases={4: 1},
    )


def store_kernel(where, plan, place, *refs):
    terms, out, sem = refs[:4], refs[5], refs[6]
    columns = terms[0].shape[1]

    @pl.when(plan[where.section] == plan[where.back + place[0]])
    def _():
        copies = [
            pltpu.make_async_copy(
                term, out.at[:, window(plan[where.section] ^ distance, columns)], sem.at[distance]
            )
            for distance, term in enumerate(terms)
        ]
        for copy in copies:
            copy.start()
        for copy in copies:
            copy.wait()


def store(where, plan, place, terms, old):
    return call(
        functools.partial(store_kernel, where),
        "store",
        (plan, place, *terms, old),
        [smem, smem] + [anywhere] * 5,
        shaped(old.shape),
        anywhere,
        scratch_shapes=[pltpu.SemaphoreType.DMA((4,))],
        input_output_aliases={6: 0},
    )


def from_sections(block):
    beside = swap(block, "section", 1)
    over = swap(block, "section", 2)
    return [block, beside, over, swap(over, "section", 1)]


def to_sections(blocks):
    return jnp.stack([blocks[0]] + [swap(blocks[k], "section", k) for k in (1, 2, 3)])


def from_groups(block):
    line = [block] + [swap(block, "fsdp", bits) for bits in (2, 4, 6)]
    other = [swap(b, "fsdp", 1) for b in line]
    return jnp.stack([b for pair in zip(line, other) for b in pair])


def sum_halves(stay, go, axis):
    near = add(stay, swap(go, axis, 1)).astype(bf16)
    total = near[0].astype(f32)
    for k in range(1, near.shape[0]):
        total = total + swap(near[k], axis, 2 * k).astype(f32)
    return total.astype(bf16)


def after(first, *later):
    return lax.optimization_barrier((first, *later))


def on_four_by_eight(
    student_w, teacher_w, saved_in, saved_pre, cotangent, slot_order, layer_counts, teacher_in
):
    sections = lax.axis_size("section")
    groups = lax.axis_size("fsdp")
    slots, tokens, width = cotangent.shape
    student = student_w[0, 0]
    deep, wide = student.shape
    rows = slots * tokens
    part = rows // sections
    part_f = teacher_in.shape[0] * tokens // sections
    scale = 1.0 / math.sqrt(rows * groups)
    where = Plan(sections)
    plan = make_plan(where, layer_counts)
    inputs_own = saved_in[0, 0].reshape(sections, part, width)
    pre_own = saved_pre[0, 0].reshape(sections, part, wide)

    def stage(place, grad, hidden, slopes, inputs, outs, spreads):
        weight, low, saved = spreads
        outs_grad, outs_hidden, weight_grad = outs
        feats = lax.all_to_all(features(inputs, hidden, groups), "fsdp", 0, 0, tiled=True)
        low_came, weight_came = across(
            where, plan, place, (where.ahead, where.back), (low, weight)
        )
        feats = jnp.stack(from_sections(feats))
        slopes = from_groups(slopes)
        pre = ahead_product(where, part, plan, place, feats, *low, low_came)
        pre = to_sections(sum_halves(*pre, "fsdp"))
        hidden, outs_hidden = update_hidden(where, plan, place, hidden, pre, outs_hidden)
        dn = back_product(where, plan, place, slopes, *weight, weight_came)
        dn = lax.all_to_all(sum_halves(*dn, "section"), "fsdp", 0, 0, tiled=True)
        grad, outs_grad = update(where, plan, place, grad, inputs, dn, outs_grad)
        terms = from_sections(grad_product(where, scale, plan, feats, slopes))
        weight_grad = store(where, plan, place, terms, weight_grad)
        (came,) = across(where, plan, place + 1, (where.back,), (saved,))
        inputs, pre = take_rows(where, plan, place + 1, *saved, came)
        return grad, hidden, inputs, pre, (outs_grad, outs_hidden, weight_grad)

    first = jnp.zeros((1,), jnp.int32)
    near, far, grad = first_slopes(where, plan, slot_order, cotangent, pre_own)
    far = swap(far, "section", 1)
    (came,) = across(where, plan, first, (where.back,), ((near, far),))
    slopes = choose(where, plan, near, far, came)
    fed = teacher_in.reshape(sections, part_f, width)
    hidden = lax.dynamic_slice(
        teacher_in.reshape(-1, width),
        (lax.axis_index("section") * part_f, 0),
        (part_f, width),
        allow_negative_indices=False,
    )
    near, far = split_rows(where, plan, inputs_own, pre_own)
    saved = (near, swap(far, "section", 1))
    (came,) = across(where, plan, first, (where.back,), (saved,))
    inputs, _ = take_rows(where, plan, first, *saved, came)
    teacher_new, s_near, s_far, t_near, t_far = split_weights(
        where, plan, student, teacher_w[0, 0], sections
    )
    spreads = ((s_near, swap(s_far, "section", 1)), (t_near, swap(t_far, "section", 1)), saved)
    outs = (
        jnp.broadcast_to(grad, (sections,) + grad.shape),
        jnp.broadcast_to(hidden, (sections,) + hidden.shape),
        jnp.zeros((deep, wide), bf16),
    )
    grad, hidden, inputs, pre, outs = stage(first, grad, hidden, slopes, inputs, outs, spreads)

    def next_stage(carry):
        place, grad, hidden, inputs, pre, outs = carry
        slopes = to_sections(slope_blocks(where, plan, grad, pre, sections))
        grad, hidden, inputs, pre, outs = stage(
            place[None], grad, hidden, slopes, inputs, outs, spreads
        )
        return place + 1, grad, hidden, inputs, pre, outs

    total = plan[where.total]
    carry = (jnp.int32(1), grad, hidden, inputs, pre, outs)
    outs = lax.while_loop(lambda c: c[0] < total, next_stage, carry)[-1]
    seen = lax.all_to_all(jnp.concatenate(outs[:2], axis=1), "section", 0, 0, tiled=True)
    return (
        seen[:, :part].reshape((1,) + cotangent.shape),
        outs[2][None, None],
        teacher_new[None, None],
        seen[:, part:].reshape((1,) + teacher_in.shape),
    )


def solution(mesh):
    in_specs = (
        P("section", None, "fsdp", None),
        P("section", None, "fsdp", None),
        P("section", None, None, "fsdp", None),
        P("section", None, None, "fsdp", None),
        P(None, "fsdp", None),
        P(),
        P(),
        P(None, "fsdp", None),
    )
    out_specs = (
        P("section", None, "fsdp", None),
        P("section", None, "fsdp", None),
        P("section", None, "fsdp", None),
        P("section", None, "fsdp", None),
    )
    sizes = dict(mesh.shape)
    fits = sizes["section"] == 4 and sizes["fsdp"] == 8
    return jax.shard_map(
        on_four_by_eight if fits else on_any_mesh, mesh=mesh, in_specs=in_specs, out_specs=out_specs, check_vma=False
    )
```

```python
import functools
import math

import jax
import jax.numpy as jnp
from jax import lax
from jax.experimental import pallas as pl
from jax.experimental.pallas import tpu as pltpu
from jax.sharding import PartitionSpec as P

epsilon = 1e-06
momentum = 0.996
f32 = jnp.float32
bf16 = jnp.bfloat16


def swap(block, axis, bits):
    size = lax.axis_size(axis)
    return lax.ppermute(block, axis, [(i, i ^ bits) for i in range(size)])


def reorder(blocks, axis):
    me = lax.axis_index(axis)
    return jnp.stack(
        [lax.dynamic_index_in_dim(blocks, me ^ j, 0, False) for j in range(blocks.shape[0])]
    )


def gather(block, axis):
    return reorder(lax.all_gather(block, axis, axis=0), axis)


def exchange(blocks, axis):
    return lax.all_to_all(blocks, axis, split_axis=0, concat_axis=0, tiled=True)


def exchange_near(blocks, axis):
    return reorder(exchange(reorder(blocks, axis), axis), axis)


def add(a, b):
    return a.astype(f32) + b.astype(f32)


def reduce_near(blocks, axis):
    return jnp.sum(exchange_near(blocks, axis).astype(f32), axis=0)


def scatter_from(root, block_at):
    size = lax.axis_size("section")
    blocks = exchange(jnp.stack([block_at(j) for j in range(size)]), "section")
    return lax.dynamic_index_in_dim(blocks, root, 0, False)


def normalize(values):
    wide = values.astype(f32)
    factor = lax.rsqrt(jnp.mean(wide * wide, axis=-1, keepdims=True) + epsilon)
    return (wide * factor, factor)


def gelu_slope(pre):
    wide = pre.astype(f32)
    return 0.5 * (1.0 + lax.erf(wide / math.sqrt(2.0))) + wide * jnp.exp(
        -0.5 * wide * wide
    ) / math.sqrt(2.0 * math.pi)


def times_slope(incoming, pre):
    return (incoming.astype(f32) * gelu_slope(pre)).astype(bf16)


def on_any_mesh(
    student_w, teacher_w, saved_in, saved_pre, cotangent, slot_order, layer_counts, teacher_in
):
    sections = lax.axis_size("section")
    groups = lax.axis_size("fsdp")
    section_id = lax.axis_index("section")
    slots, tokens, width = cotangent.shape
    student = student_w[0, 0]
    deep, wide = student.shape
    columns = wide // sections
    rows = slots * tokens
    part = rows // sections
    rows_f = teacher_in.shape[0] * tokens
    part_f = rows_f // sections
    inputs_own = saved_in[0, 0].reshape(rows, width)
    pre_own = saved_pre[0, 0].reshape(rows, wide)
    scale = 1.0 / math.sqrt(rows * groups)

    active = layer_counts > 0
    flags = active.astype(jnp.int32)
    total = jnp.sum(flags)
    up_to = jnp.cumsum(flags)
    ids = jnp.arange(sections)

    def met(place):
        back = jnp.sum(jnp.where(active & (total - up_to == place), ids, 0))
        ahead = jnp.sum(jnp.where(active & (up_to - 1 == place), ids, 0))
        return back, ahead

    done_back = jnp.sum(jnp.where(ids >= section_id, flags, 0))
    done_ahead = jnp.sum(jnp.where(ids <= section_id, flags, 0))

    teacher_new = momentum * teacher_w[0, 0] + (1.0 - momentum) * student.astype(f32)
    teacher_low = teacher_new.astype(bf16)

    def column_block(array):
        return lambda j: lax.dynamic_slice_in_dim(array, j * columns, columns, 1)

    def row_block(array, count):
        return lambda j: lax.dynamic_slice_in_dim(array, j * count, count, 0)

    def to_features(values):
        blocks = values.reshape(values.shape[0], groups, deep).transpose(1, 0, 2)
        return reorder(exchange(blocks, "fsdp"), "fsdp")

    def stage(place, grad, hidden, slopes):
        back, ahead = met(place)
        normed_h, _ = normalize(hidden)
        feats_h = gather(to_features(normed_h.astype(bf16)), "section")
        teacher = scatter_from(ahead, column_block(teacher_low))
        pre = jnp.dot(
            feats_h.reshape(-1, deep), teacher, preferred_element_type=f32
        ).astype(bf16)
        pre = pre.reshape(sections, groups, part_f, columns).transpose(1, 0, 2, 3)
        pre = reduce_near(pre, "fsdp").astype(bf16)
        pre = reorder(exchange_near(pre, "section"), "section")
        pre = pre.transpose(1, 0, 2).reshape(part_f, wide).astype(f32)
        hidden = (hidden.astype(f32) + jax.nn.gelu(pre, approximate=False)).astype(bf16)
        inputs = scatter_from(back, row_block(inputs_own, part))
        weight = scatter_from(back, column_block(student))
        slopes = gather(slopes, "fsdp").reshape(-1, columns)
        dn = lax.dot_general(
            slopes, weight, (((1,), (1,)), ((), ())), preferred_element_type=f32
        ).astype(bf16)
        dn = dn.reshape(groups, sections, part, deep).transpose(1, 0, 2, 3)
        dn = reduce_near(dn, "section").astype(bf16)
        dn = exchange(reorder(dn, "fsdp"), "fsdp")
        dn = dn.transpose(1, 0, 2).reshape(part, width).astype(f32)
        normed, factor = normalize(inputs)
        grad = (
            grad.astype(f32)
            + factor * (dn - normed * jnp.mean(dn * normed, axis=-1, keepdims=True))
        ).astype(bf16)
        feats = gather(to_features(normed.astype(bf16)), "section").transpose(1, 0, 2, 3)
        term = lax.dot_general(
            feats.reshape(-1, deep), slopes, (((0,), (0,)), ((), ())), preferred_element_type=f32
        )
        term = reorder(gather((scale * term).astype(bf16), "section"), "section")
        return grad, hidden, term.transpose(1, 0, 2).reshape(deep, wide), back

    def publish(grad, hidden):
        both = reorder(gather(jnp.concatenate([grad, hidden]), "section"), "section")
        return both[:, :part].reshape(rows, width), both[:, part:].reshape(rows_f, width)

    cot = jnp.stack([cotangent[slot_order[k]] for k in range(slots)]).reshape(rows, width)
    fed = teacher_in.reshape(rows_f, width)
    grad = row_block(cot, part)(section_id)
    hidden = row_block(fed, part_f)(section_id)
    slopes = scatter_from(met(0)[0], column_block(times_slope(cot, pre_own)))
    slopes = reorder(slopes.reshape(sections, part, columns), "section")
    grad, hidden, term, back = stage(0, grad, hidden, slopes)
    weight_grad = jnp.where(section_id == back, term, jnp.zeros_like(term))

    def next_stage(place, operands):
        grad, hidden, out_grad, out_hidden, weight_grad = operands
        seen_grad, seen_hidden = publish(grad, hidden)
        out_grad = jnp.where(done_back == place, seen_grad, out_grad)
        out_hidden = jnp.where(done_ahead == place, seen_hidden, out_hidden)
        pre = scatter_from(met(place)[0], row_block(pre_own, part))
        slopes = times_slope(grad, pre).reshape(part, sections, columns).transpose(1, 0, 2)
        slopes = exchange_near(reorder(slopes, "section"), "section")
        grad, hidden, term, back = stage(place, grad, hidden, slopes)
        weight_grad = jnp.where(section_id == back, term, weight_grad)
        return grad, hidden, out_grad, out_hidden, weight_grad

    carry = (grad, hidden, cot, fed, weight_grad)
    for place in range(1, sections - 1):
        carry = lax.cond(
            place < total, lambda c, place=place: next_stage(place, c), lambda c: c, carry
        )
    grad, hidden, out_grad, out_hidden, weight_grad = carry
    seen_grad, seen_hidden = publish(grad, hidden)
    out_grad = jnp.where(done_back == total, seen_grad, out_grad)
    out_hidden = jnp.where(done_ahead == total, seen_hidden, out_hidden)
    return (
        out_grad.reshape((1,) + cotangent.shape),
        weight_grad[None, None],
        teacher_new[None, None],
        out_hidden.reshape((1,) + teacher_in.shape),
    )


vmem = pl.BlockSpec(memory_space=pltpu.VMEM)
smem = pl.BlockSpec(memory_space=pltpu.SMEM)
anywhere = pl.BlockSpec(memory_space=pl.ANY)
in_hbm = pl.BlockSpec(memory_space=pltpu.HBM)
params = pltpu.CompilerParams(vmem_limit_bytes=40 * 2**20)


def call(body, name, operands, spaces, out_shape, out_spaces, **more):
    return pl.pallas_call(
        body,
        in_specs=spaces,
        out_specs=out_spaces,
        out_shape=out_shape,
        compiler_params=params,
        name=name,
        **more,
    )(*operands)


def shaped(shape, dtype=bf16):
    return jax.ShapeDtypeStruct(shape, dtype)


def window(block, size):
    return pl.ds(pl.multiple_of(block * size, size), size)


class Plan:
    def __init__(self, sections):
        self.section, self.group, self.total, self.back = 0, 1, 2, 3
        self.ahead = self.back + sections + 1
        self.done_back = self.ahead + sections + 1
        self.done_ahead = self.done_back + sections
        self.size = self.done_ahead + sections


def plan_kernel(where, counts_ref, section_ref, group_ref, out_ref):
    sections = counts_ref.shape[0]
    out_ref[where.section] = section_ref[0]
    out_ref[where.group] = group_ref[0]
    seen = jnp.int32(0)
    for s in range(sections):
        out_ref[where.ahead + seen] = jnp.int32(s)
        seen = seen + (counts_ref[s] > 0).astype(jnp.int32)
        out_ref[where.done_ahead + s] = seen
    out_ref[where.total] = seen
    out_ref[where.ahead + sections] = jnp.int32(0)
    seen = jnp.int32(0)
    for s in reversed(range(sections)):
        out_ref[where.back + seen] = jnp.int32(s)
        seen = seen + (counts_ref[s] > 0).astype(jnp.int32)
        out_ref[where.done_back + s] = seen
    out_ref[where.back + sections] = jnp.int32(0)


def make_plan(where, counts):
    me = [lax.axis_index(axis).astype(jnp.int32)[None] for axis in ("section", "fsdp")]
    return call(
        functools.partial(plan_kernel, where),
        "make_plan",
        (counts, *me),
        [smem] * 3,
        shaped((where.size,), jnp.int32),
        smem,
    )


def first_kernel(where, plan, order, cot, pre, near_out, far_out, grad_out):
    sections, _, columns = near_out.shape[1:]
    me = plan[where.section]
    grad_out[...] = cot[order[me]]
    for distance in range(sections):
        target = me ^ distance
        out = (near_out, far_out)[distance & 1]
        for slot in range(sections):
            out[distance >> 1, pl.ds(slot ^ target, 1)] = times_slope(
                cot[order[slot], :, window(target, columns)],
                pre[slot, :, window(target, columns)],
            )[None]


def first_slopes(where, plan, order, cot, pre):
    sections, part, wide = pre.shape
    half = shaped((sections // 2, sections, part, wide // sections))
    return call(
        functools.partial(first_kernel, where),
        "first_slopes",
        (plan, order, cot, pre),
        [smem, smem, vmem, vmem],
        [half, half, shaped((part, wide))],
        [vmem] * 3,
    )


def weights_kernel(where, plan, student_ref, teacher_ref, new_ref, s_near, s_far, t_near, t_far):
    sections, columns = 2 * s_near.shape[0], s_near.shape[2]
    new_ref[...] = momentum * teacher_ref[...] + (1.0 - momentum) * student_ref[...].astype(f32)
    for distance in range(sections):
        cols = window(plan[where.section] ^ distance, columns)
        (s_near, s_far)[distance & 1][distance >> 1] = student_ref[:, cols]
        (t_near, t_far)[distance & 1][distance >> 1] = new_ref[:, cols].astype(bf16)


def split_weights(where, plan, student, teacher, sections):
    deep, wide = student.shape
    tile = 64
    columns = wide // sections
    whole = pl.BlockSpec((tile, wide), lambda i: (i, 0))
    half = pl.BlockSpec((sections // 2, tile, columns), lambda i: (0, i, 0))
    out = shaped((sections // 2, deep, columns))
    return call(
        functools.partial(weights_kernel, where),
        "split_weights",
        (plan, student, teacher),
        [smem, whole, whole],
        [shaped(teacher.shape, f32)] + [out] * 4,
        [whole] + [half] * 4,
        grid=(deep // tile,),
    )


def rows_kernel(where, plan, inputs_ref, pre_ref, near_out, far_out):
    part = inputs_ref.shape[1]
    for distance in range(inputs_ref.shape[0]):
        target = plan[where.section] ^ distance
        out = (near_out, far_out)[distance & 1]
        out[distance >> 1, :part] = inputs_ref[target]
        out[distance >> 1, part:] = pre_ref[target]


def split_rows(where, plan, inputs, pre):
    sections, part, wide = inputs.shape
    half = shaped((sections // 2, 2 * part, wide))
    return call(
        functools.partial(rows_kernel, where),
        "split_rows",
        (plan, inputs, pre),
        [smem, vmem, vmem],
        [half, half],
        [vmem] * 2,
    )


def send_kernel(where, root_at, plan, place, *refs):
    count = len(root_at)
    outs, sem = refs[2 * count : 3 * count], refs[3 * count]
    for i, at in enumerate(root_at):
        distance = plan[where.section] ^ plan[at + place[0]]
        for core in (0, 1):

            @pl.when((distance & 1) == core)
            def _(i=i, core=core):
                pltpu.make_async_copy(refs[2 * i + core].at[1], outs[i], sem.at[i]).start()

    for i in range(count):
        pltpu.make_async_copy(refs[2 * i].at[1], outs[i], sem.at[i]).wait()


def sends(where, plan, place, roots, pairs):
    flat = [half for pair in pairs for half in pair]
    return call(
        functools.partial(send_kernel, where, tuple(roots)),
        "send_blocks",
        (plan, place, *flat),
        [smem, smem] + [anywhere] * len(flat),
        [shaped(near.shape[1:]) for near, _ in pairs],
        [vmem] * len(pairs),
        scratch_shapes=[pltpu.SemaphoreType.DMA((len(pairs),))],
    )


def across(where, plan, place, roots, pairs):
    return [swap(block, "section", 2) for block in sends(where, plan, place, roots, pairs)]


def fetch(distance, near, far, came, held, sem):
    choices = ((near.at[0], 0), (far.at[0], 1), (came, 2), (came, 3))
    for source, at in choices:

        @pl.when(distance == at)
        def _(source=source):
            pltpu.make_async_copy(source, held, sem).start()

    pltpu.make_async_copy(came, held, sem).wait()


def take_kernel(where, plan, place, near, far, came, inputs_out, pre_out, sem):
    distance = plan[where.section] ^ plan[where.back + place[0]]
    part = inputs_out.shape[0]
    for j, out in enumerate((inputs_out, pre_out)):
        rows = pl.ds(j * part, part)
        for source, at in ((near.at[0], 0), (far.at[0], 1), (came, 2), (came, 3)):

            @pl.when(distance == at)
            def _(source=source, out=out, rows=rows, j=j):
                pltpu.make_async_copy(source.at[rows], out, sem.at[j]).start()

    for j, out in enumerate((inputs_out, pre_out)):
        pltpu.make_async_copy(came.at[pl.ds(j * part, part)], out, sem.at[j]).wait()


def take_rows(where, plan, place, near, far, came):
    part = came.shape[0] // 2
    return call(
        functools.partial(take_kernel, where),
        "take_rows",
        (plan, place, near, far, came),
        [smem, smem] + [anywhere] * 3,
        [shaped((part, came.shape[1]))] * 2,
        [vmem] * 2,
        scratch_shapes=[pltpu.SemaphoreType.DMA((2,))],
    )


def choose_kernel(where, plan, near, far, came, out, sem):
    distance = plan[where.section] ^ plan[where.back]
    fetch(distance, near, far, came, out, sem)


def choose(where, plan, near, far, came):
    return call(
        functools.partial(choose_kernel, where),
        "choose",
        (plan, near, far, came),
        [smem] + [anywhere] * 3,
        shaped(came.shape),
        vmem,
        scratch_shapes=[pltpu.SemaphoreType.DMA],
    )


def features_kernel(inputs_ref, hidden_ref, out_ref):
    groups, _, deep = out_ref.shape
    part = inputs_ref.shape[0]
    for rows, ref in ((pl.ds(0, part), inputs_ref), (pl.ds(part, hidden_ref.shape[0]), hidden_ref)):
        normed = normalize(ref[...])[0].astype(bf16)
        for j in range(groups):
            out_ref[j, rows] = normed[:, j * deep : (j + 1) * deep]


def features(inputs, hidden, groups):
    rows = inputs.shape[0] + hidden.shape[0]
    return call(
        features_kernel,
        "features",
        (inputs, hidden),
        [vmem, vmem],
        shaped((groups, rows, inputs.shape[1] // groups)),
        vmem,
    )


def back_kernel(where, plan, place, slopes_ref, near, far, came, stay_out, go_out, weight, sem):
    groups, sections, part, columns = slopes_ref.shape
    distance = plan[where.section] ^ plan[where.back + place[0]]
    fetch(distance, near, far, came, weight, sem)
    for k in range(groups):
        dn = lax.dot_general(
            slopes_ref[k].reshape(sections * part, columns),
            weight[...],
            (((1,), (1,)), ((), ())),
            preferred_element_type=f32,
        ).astype(bf16)
        dn = dn.reshape(sections, part, weight.shape[0])
        for s in range(sections):
            out = (stay_out, go_out)[s & 1]
            out[s >> 1, pl.ds(plan[where.group] ^ k, 1)] = dn[s][None]


def back_product(where, plan, place, slopes, near, far, came):
    groups, sections, part, _ = slopes.shape
    out = shaped((sections // 2, groups, part, came.shape[0]))
    return call(
        functools.partial(back_kernel, where),
        "back_product",
        (plan, place, slopes, near, far, came),
        [smem, smem, vmem] + [anywhere] * 3,
        [out, out],
        [vmem] * 2,
        scratch_shapes=[pltpu.VMEM(came.shape, bf16), pltpu.SemaphoreType.DMA],
    )


def ahead_kernel(where, part, plan, place, feats_ref, near, far, came, stay_out, go_out, weight, sem):
    sections, groups, rows, deep = feats_ref.shape
    part_f, columns = rows - part, came.shape[1]
    distance = plan[where.section] ^ plan[where.ahead + place[0]]
    fetch(distance, near, far, came, weight, sem)
    side = plan[where.group] & 1
    for s in range(sections):
        pre = jnp.dot(
            feats_ref[s, :, part:, :].reshape(groups * part_f, deep),
            weight[...],
            preferred_element_type=f32,
        ).astype(bf16)
        pre = pre.reshape(groups, part_f, columns)
        for j in range(0, groups, 2):
            seat = (plan[where.group] ^ j) >> 1
            stay_out[pl.ds(seat, 1), s] = jnp.where(side == 0, pre[j], pre[j + 1])[None]
            go_out[pl.ds(seat, 1), s] = jnp.where(side == 0, pre[j + 1], pre[j])[None]


def ahead_product(where, part, plan, place, feats, near, far, came):
    sections, groups, rows, _ = feats.shape
    out = shaped((groups // 2, sections, rows - part, came.shape[1]))
    return call(
        functools.partial(ahead_kernel, where, part),
        "ahead_product",
        (plan, place, feats, near, far, came),
        [smem, smem, vmem] + [anywhere] * 3,
        [out, out],
        [vmem] * 2,
        scratch_shapes=[pltpu.VMEM(came.shape, bf16), pltpu.SemaphoreType.DMA],
    )


def grad_kernel(where, scale, plan, feats_ref, slopes_ref, out_ref, total_ref):
    groups, sections, part, columns = slopes_ref.shape
    deep = feats_ref.shape[3]
    for k in range(groups):
        feats = feats_ref[:, pl.ds(plan[where.group] ^ k, 1), :part, :]
        term = lax.dot_general(
            feats.reshape(sections * part, deep),
            slopes_ref[k].reshape(sections * part, columns),
            (((0,), (0,)), ((), ())),
            preferred_element_type=f32,
        )
        if k == 0:
            total_ref[...] = term
        else:
            total_ref[...] += term
    out_ref[...] = (scale * total_ref[...]).astype(bf16)


def grad_product(where, scale, plan, feats, slopes):
    size = (feats.shape[3], slopes.shape[3])
    return call(
        functools.partial(grad_kernel, where, scale),
        "grad_product",
        (plan, feats, slopes),
        [smem, vmem, vmem],
        shaped(size),
        vmem,
        scratch_shapes=[pltpu.VMEM(size, f32)],
    )


def slopes_kernel(where, plan, grad_ref, pre_ref, out_ref):
    sections, _, columns = out_ref.shape
    for distance in range(sections):
        cols = window(plan[where.section] ^ distance, columns)
        out_ref[distance] = times_slope(grad_ref[:, cols], pre_ref[:, cols])


def slope_blocks(where, plan, grad, pre, sections):
    part, wide = pre.shape
    return call(
        functools.partial(slopes_kernel, where),
        "slope_blocks",
        (plan, grad, pre),
        [smem, vmem, vmem],
        shaped((sections, part, wide // sections)),
        vmem,
    )


def write_seen(done, sections, plan, place, values, outs, sem):
    for start in (True, False):
        for s in range(sections):

            @pl.when(plan[done + s] == place[0] + 1)
            def _(s=s, start=start):
                copy = pltpu.make_async_copy(values, outs.at[s], sem.at[s])
                copy.start() if start else copy.wait()


def update_kernel(where, plan, place, grad_ref, inputs_ref, dn_ref, old, out_ref, outs, sem):
    groups = dn_ref.shape[0]
    dn = jnp.concatenate([dn_ref[j].astype(f32) for j in range(groups)], axis=1)
    normed, factor = normalize(inputs_ref[...])
    grad = grad_ref[...].astype(f32) + factor * (
        dn - normed * jnp.mean(dn * normed, axis=-1, keepdims=True)
    )
    out_ref[...] = grad.astype(bf16)
    write_seen(where.done_back, old.shape[0], plan, place, out_ref, outs, sem)


def update(where, plan, place, grad, inputs, dn, outs):
    return call(
        functools.partial(update_kernel, where),
        "update",
        (plan, place, grad, inputs, dn, outs),
        [smem, smem, vmem, vmem, vmem, anywhere],
        [shaped(grad.shape), shaped(outs.shape)],
        [vmem, anywhere],
        scratch_shapes=[pltpu.SemaphoreType.DMA((outs.shape[0],))],
        input_output_aliases={5: 1},
    )


def hidden_kernel(where, plan, place, hidden_ref, pre_ref, old, out_ref, outs, sem):
    sections, _, columns = pre_ref.shape
    for distance in range(sections):
        cols = window(plan[where.section] ^ distance, columns)
        pre = pre_ref[distance].astype(f32)
        gelu = 0.5 * pre * (1.0 + lax.erf(pre / math.sqrt(2.0)))
        out_ref[:, cols] = (hidden_ref[:, cols].astype(f32) + gelu).astype(bf16)
    write_seen(where.done_ahead, old.shape[0], plan, place, out_ref, outs, sem)


def update_hidden(where, plan, place, hidden, pre, outs):
    return call(
        functools.partial(hidden_kernel, where),
        "update_hidden",
        (plan, place, hidden, pre, outs),
        [smem, smem, vmem, vmem, anywhere],
        [shaped(hidden.shape), shaped(outs.shape)],
        [vmem, anywhere],
        scratch_shapes=[pltpu.SemaphoreType.DMA((outs.shape[0],))],
        input_output_aliases={4: 1},
    )


def store_kernel(where, plan, place, *refs):
    terms, out, sem = refs[:4], refs[5], refs[6]
    columns = terms[0].shape[1]

    @pl.when(plan[where.section] == plan[where.back + place[0]])
    def _():
        copies = [
            pltpu.make_async_copy(
                term, out.at[:, window(plan[where.section] ^ distance, columns)], sem.at[distance]
            )
            for distance, term in enumerate(terms)
        ]
        for copy in copies:
            copy.start()
        for copy in copies:
            copy.wait()


def store(where, plan, place, terms, old):
    return call(
        functools.partial(store_kernel, where),
        "store",
        (plan, place, *terms, old),
        [smem, smem] + [anywhere] * 5,
        shaped(old.shape),
        anywhere,
        scratch_shapes=[pltpu.SemaphoreType.DMA((4,))],
        input_output_aliases={6: 0},
    )


def pack_kernel(where, plan, grads, hiddens, *refs):
    outs, sem = refs[:-1], refs[-1]
    part = grads.shape[1]
    for wait in (False, True):
        for distance, out in enumerate(outs):
            target = plan[where.section] ^ distance
            for j, (source, rows) in enumerate(
                ((grads, pl.ds(0, part)), (hiddens, pl.ds(part, hiddens.shape[1])))
            ):
                copy = pltpu.make_async_copy(source.at[target], out.at[rows], sem.at[2 * distance + j])
                copy.wait() if wait else copy.start()


def pack(where, plan, grads, hiddens):
    sections, part, width = grads.shape
    out = shaped((part + hiddens.shape[1], width))
    return call(
        functools.partial(pack_kernel, where),
        "pack",
        (plan, grads, hiddens),
        [smem, anywhere, anywhere],
        [out] * sections,
        [vmem] * sections,
        scratch_shapes=[pltpu.SemaphoreType.DMA((2 * sections,))],
    )


def unpack_kernel(where, plan, *refs):
    pieces, (grads, hiddens, sem) = refs[:-3], refs[-3:]
    part = grads.shape[1]
    for wait in (False, True):
        for distance, piece in enumerate(pieces):
            source = plan[where.section] ^ distance
            for j, (out, rows) in enumerate(
                ((grads, pl.ds(0, part)), (hiddens, pl.ds(part, hiddens.shape[1])))
            ):
                copy = pltpu.make_async_copy(piece.at[rows], out.at[source], sem.at[2 * distance + j])
                copy.wait() if wait else copy.start()


def unpack(where, plan, pieces, part):
    rows, width = pieces[0].shape
    return call(
        functools.partial(unpack_kernel, where),
        "unpack",
        (plan, *pieces),
        [smem] + [anywhere] * len(pieces),
        [shaped((len(pieces), part, width)), shaped((len(pieces), rows - part, width))],
        [in_hbm] * 2,
        scratch_shapes=[pltpu.SemaphoreType.DMA((2 * len(pieces),))],
    )


def from_sections(block):
    beside = swap(block, "section", 1)
    over = swap(block, "section", 2)
    return [block, beside, over, swap(over, "section", 1)]


def to_sections(blocks):
    return jnp.stack([blocks[0]] + [swap(blocks[k], "section", k) for k in (1, 2, 3)])


def from_groups(block):
    line = [block] + [swap(block, "fsdp", bits) for bits in (2, 4, 6)]
    other = [swap(b, "fsdp", 1) for b in line]
    return jnp.stack([b for pair in zip(line, other) for b in pair])


def sum_halves(stay, go, axis):
    near = add(stay, swap(go, axis, 1)).astype(bf16)
    total = near[0].astype(f32)
    for k in range(1, near.shape[0]):
        total = total + swap(near[k], axis, 2 * k).astype(f32)
    return total.astype(bf16)


def fence(*values):
    return lax.optimization_barrier(values)


def on_four_by_eight(
    student_w, teacher_w, saved_in, saved_pre, cotangent, slot_order, layer_counts, teacher_in
):
    sections = lax.axis_size("section")
    groups = lax.axis_size("fsdp")
    slots, tokens, width = cotangent.shape
    student = student_w[0, 0]
    deep, wide = student.shape
    rows = slots * tokens
    part = rows // sections
    part_f = teacher_in.shape[0] * tokens // sections
    scale = 1.0 / math.sqrt(rows * groups)
    where = Plan(sections)
    plan = make_plan(where, layer_counts)
    inputs_own = saved_in[0, 0].reshape(sections, part, width)
    pre_own = saved_pre[0, 0].reshape(sections, part, wide)

    def to_groups(blocks):
        return lax.all_to_all(blocks, "fsdp", 0, 0, tiled=True)

    def stage(place, grad, hidden, slopes, inputs, outs, spreads, first=False):
        weight, low, saved = spreads
        outs_grad, outs_hidden, weight_grad = outs
        if first:
            feats = to_groups(features(inputs, hidden, groups))
            feats, slopes = fence(feats, slopes)
            came = across(where, plan, place, (where.ahead, where.back), (low, weight))
            slopes = from_groups(slopes)
        else:
            came = across(where, plan, place, (where.ahead, where.back), (low, weight))
            line = [slopes] + [swap(slopes, "fsdp", bits) for bits in (2, 4, 6)]
            line[1], line[3], inputs, hidden = fence(line[1], line[3], inputs, hidden)
            feats = to_groups(features(inputs, hidden, groups))
            slopes = jnp.stack([b for near in line for b in (near, swap(near, "fsdp", 1))])
        low_came, weight_came = came
        feats = jnp.stack(from_sections(feats))
        pre = ahead_product(where, part, plan, place, feats, *low, low_came)
        pre = to_sections(sum_halves(*pre, "fsdp"))
        hidden, outs_hidden = update_hidden(where, plan, place, hidden, pre, outs_hidden)
        dn = back_product(where, plan, place, slopes, *weight, weight_came)
        dn = lax.all_to_all(sum_halves(*dn, "section"), "fsdp", 0, 0, tiled=True)
        grad, outs_grad = update(where, plan, place, grad, inputs, dn, outs_grad)
        terms = from_sections(grad_product(where, scale, plan, feats, slopes))
        weight_grad = store(where, plan, place, terms, weight_grad)
        (came,) = across(where, plan, place + 1, (where.back,), (saved,))
        inputs, pre = take_rows(where, plan, place + 1, *saved, came)
        return grad, hidden, inputs, pre, (outs_grad, outs_hidden, weight_grad)

    first = jnp.zeros((1,), jnp.int32)
    near, far, grad = first_slopes(where, plan, slot_order, cotangent, pre_own)
    far = swap(far, "section", 1)
    (came,) = across(where, plan, first, (where.back,), ((near, far),))
    slopes = choose(where, plan, near, far, came)
    hidden = lax.dynamic_slice(
        teacher_in.reshape(-1, width),
        (lax.axis_index("section") * part_f, 0),
        (part_f, width),
        allow_negative_indices=False,
    )
    near, far = split_rows(where, plan, inputs_own, pre_own)
    saved = (near, swap(far, "section", 1))
    (came,) = across(where, plan, first, (where.back,), (saved,))
    inputs, _ = take_rows(where, plan, first, *saved, came)
    teacher_new, s_near, s_far, t_near, t_far = split_weights(
        where, plan, student, teacher_w[0, 0], sections
    )
    spreads = ((s_near, swap(s_far, "section", 1)), (t_near, swap(t_far, "section", 1)), saved)
    outs = (
        jnp.broadcast_to(grad, (sections,) + grad.shape),
        jnp.broadcast_to(hidden, (sections,) + hidden.shape),
        jnp.zeros((deep, wide), bf16),
    )
    grad, hidden, inputs, pre, outs = stage(
        first, grad, hidden, slopes, inputs, outs, spreads, True
    )

    def next_stage(carry):
        place, grad, hidden, inputs, pre, outs = carry
        slopes = to_sections(slope_blocks(where, plan, grad, pre, sections))
        grad, hidden, inputs, pre, outs = stage(
            place[None], grad, hidden, slopes, inputs, outs, spreads
        )
        return place + 1, grad, hidden, inputs, pre, outs

    total = plan[where.total]
    carry = (jnp.int32(1), grad, hidden, inputs, pre, outs)
    outs = lax.while_loop(lambda c: c[0] < total, next_stage, carry)[-1]
    blocks = pack(where, plan, *outs[:2])
    pieces = [blocks[0]] + [swap(blocks[k], "section", k) for k in (1, 2, 3)]
    input_grad, teacher_out = unpack(where, plan, pieces, part)
    return (
        input_grad.reshape((1,) + cotangent.shape),
        outs[2][None, None],
        teacher_new[None, None],
        teacher_out.reshape((1,) + teacher_in.shape),
    )


def solution(mesh):
    in_specs = (
        P("section", None, "fsdp", None),
        P("section", None, "fsdp", None),
        P("section", None, None, "fsdp", None),
        P("section", None, None, "fsdp", None),
        P(None, "fsdp", None),
        P(),
        P(),
        P(None, "fsdp", None),
    )
    out_specs = (
        P("section", None, "fsdp", None),
        P("section", None, "fsdp", None),
        P("section", None, "fsdp", None),
        P("section", None, "fsdp", None),
    )
    sizes = dict(mesh.shape)
    fits = sizes["section"] == 4 and sizes["fsdp"] == 8
    return jax.shard_map(
        on_four_by_eight if fits else on_any_mesh, mesh=mesh, in_specs=in_specs, out_specs=out_specs, check_vma=False
    )
```

```python
import functools
import math

import jax
import jax.numpy as jnp
from jax import lax
from jax.experimental import pallas as pl
from jax.experimental.pallas import tpu as pltpu
from jax.sharding import PartitionSpec as P

epsilon = 1e-06
momentum = 0.996
f32 = jnp.float32
bf16 = jnp.bfloat16


def swap(block, axis, bits):
    size = lax.axis_size(axis)
    return lax.ppermute(block, axis, [(i, i ^ bits) for i in range(size)])


def reorder(blocks, axis):
    me = lax.axis_index(axis)
    return jnp.stack(
        [lax.dynamic_index_in_dim(blocks, me ^ j, 0, False) for j in range(blocks.shape[0])]
    )


def gather(block, axis):
    return reorder(lax.all_gather(block, axis, axis=0), axis)


def exchange(blocks, axis):
    return lax.all_to_all(blocks, axis, split_axis=0, concat_axis=0, tiled=True)


def exchange_near(blocks, axis):
    return reorder(exchange(reorder(blocks, axis), axis), axis)


def add(a, b):
    return a.astype(f32) + b.astype(f32)


def reduce_near(blocks, axis):
    return jnp.sum(exchange_near(blocks, axis).astype(f32), axis=0)


def scatter_from(root, block_at):
    size = lax.axis_size("section")
    blocks = exchange(jnp.stack([block_at(j) for j in range(size)]), "section")
    return lax.dynamic_index_in_dim(blocks, root, 0, False)


def normalize(values):
    wide = values.astype(f32)
    factor = lax.rsqrt(jnp.mean(wide * wide, axis=-1, keepdims=True) + epsilon)
    return (wide * factor, factor)


def gelu_slope(pre):
    wide = pre.astype(f32)
    return 0.5 * (1.0 + lax.erf(wide / math.sqrt(2.0))) + wide * jnp.exp(
        -0.5 * wide * wide
    ) / math.sqrt(2.0 * math.pi)


def times_slope(incoming, pre):
    return (incoming.astype(f32) * gelu_slope(pre)).astype(bf16)


def on_any_mesh(
    student_w, teacher_w, saved_in, saved_pre, cotangent, slot_order, layer_counts, teacher_in
):
    sections = lax.axis_size("section")
    groups = lax.axis_size("fsdp")
    section_id = lax.axis_index("section")
    slots, tokens, width = cotangent.shape
    student = student_w[0, 0]
    deep, wide = student.shape
    columns = wide // sections
    rows = slots * tokens
    part = rows // sections
    rows_f = teacher_in.shape[0] * tokens
    part_f = rows_f // sections
    inputs_own = saved_in[0, 0].reshape(rows, width)
    pre_own = saved_pre[0, 0].reshape(rows, wide)
    scale = 1.0 / math.sqrt(rows * groups)

    active = layer_counts > 0
    flags = active.astype(jnp.int32)
    total = jnp.sum(flags)
    up_to = jnp.cumsum(flags)
    ids = jnp.arange(sections)

    def met(place):
        back = jnp.sum(jnp.where(active & (total - up_to == place), ids, 0))
        ahead = jnp.sum(jnp.where(active & (up_to - 1 == place), ids, 0))
        return back, ahead

    done_back = jnp.sum(jnp.where(ids >= section_id, flags, 0))
    done_ahead = jnp.sum(jnp.where(ids <= section_id, flags, 0))

    teacher_new = momentum * teacher_w[0, 0] + (1.0 - momentum) * student.astype(f32)
    teacher_low = teacher_new.astype(bf16)

    def column_block(array):
        return lambda j: lax.dynamic_slice_in_dim(array, j * columns, columns, 1)

    def row_block(array, count):
        return lambda j: lax.dynamic_slice_in_dim(array, j * count, count, 0)

    def to_features(values):
        blocks = values.reshape(values.shape[0], groups, deep).transpose(1, 0, 2)
        return reorder(exchange(blocks, "fsdp"), "fsdp")

    def stage(place, grad, hidden, slopes):
        back, ahead = met(place)
        normed_h, _ = normalize(hidden)
        feats_h = gather(to_features(normed_h.astype(bf16)), "section")
        teacher = scatter_from(ahead, column_block(teacher_low))
        pre = jnp.dot(
            feats_h.reshape(-1, deep), teacher, preferred_element_type=f32
        ).astype(bf16)
        pre = pre.reshape(sections, groups, part_f, columns).transpose(1, 0, 2, 3)
        pre = reduce_near(pre, "fsdp").astype(bf16)
        pre = reorder(exchange_near(pre, "section"), "section")
        pre = pre.transpose(1, 0, 2).reshape(part_f, wide).astype(f32)
        hidden = (hidden.astype(f32) + jax.nn.gelu(pre, approximate=False)).astype(bf16)
        inputs = scatter_from(back, row_block(inputs_own, part))
        weight = scatter_from(back, column_block(student))
        slopes = gather(slopes, "fsdp").reshape(-1, columns)
        dn = lax.dot_general(
            slopes, weight, (((1,), (1,)), ((), ())), preferred_element_type=f32
        ).astype(bf16)
        dn = dn.reshape(groups, sections, part, deep).transpose(1, 0, 2, 3)
        dn = reduce_near(dn, "section").astype(bf16)
        dn = exchange(reorder(dn, "fsdp"), "fsdp")
        dn = dn.transpose(1, 0, 2).reshape(part, width).astype(f32)
        normed, factor = normalize(inputs)
        grad = (
            grad.astype(f32)
            + factor * (dn - normed * jnp.mean(dn * normed, axis=-1, keepdims=True))
        ).astype(bf16)
        feats = gather(to_features(normed.astype(bf16)), "section").transpose(1, 0, 2, 3)
        term = lax.dot_general(
            feats.reshape(-1, deep), slopes, (((0,), (0,)), ((), ())), preferred_element_type=f32
        )
        term = reorder(gather((scale * term).astype(bf16), "section"), "section")
        return grad, hidden, term.transpose(1, 0, 2).reshape(deep, wide), back

    def publish(grad, hidden):
        both = reorder(gather(jnp.concatenate([grad, hidden]), "section"), "section")
        return both[:, :part].reshape(rows, width), both[:, part:].reshape(rows_f, width)

    cot = jnp.stack([cotangent[slot_order[k]] for k in range(slots)]).reshape(rows, width)
    fed = teacher_in.reshape(rows_f, width)
    grad = row_block(cot, part)(section_id)
    hidden = row_block(fed, part_f)(section_id)
    slopes = scatter_from(met(0)[0], column_block(times_slope(cot, pre_own)))
    slopes = reorder(slopes.reshape(sections, part, columns), "section")
    grad, hidden, term, back = stage(0, grad, hidden, slopes)
    weight_grad = jnp.where(section_id == back, term, jnp.zeros_like(term))

    def next_stage(place, operands):
        grad, hidden, out_grad, out_hidden, weight_grad = operands
        seen_grad, seen_hidden = publish(grad, hidden)
        out_grad = jnp.where(done_back == place, seen_grad, out_grad)
        out_hidden = jnp.where(done_ahead == place, seen_hidden, out_hidden)
        pre = scatter_from(met(place)[0], row_block(pre_own, part))
        slopes = times_slope(grad, pre).reshape(part, sections, columns).transpose(1, 0, 2)
        slopes = exchange_near(reorder(slopes, "section"), "section")
        grad, hidden, term, back = stage(place, grad, hidden, slopes)
        weight_grad = jnp.where(section_id == back, term, weight_grad)
        return grad, hidden, out_grad, out_hidden, weight_grad

    carry = (grad, hidden, cot, fed, weight_grad)
    for place in range(1, sections - 1):
        carry = lax.cond(
            place < total, lambda c, place=place: next_stage(place, c), lambda c: c, carry
        )
    grad, hidden, out_grad, out_hidden, weight_grad = carry
    seen_grad, seen_hidden = publish(grad, hidden)
    out_grad = jnp.where(done_back == total, seen_grad, out_grad)
    out_hidden = jnp.where(done_ahead == total, seen_hidden, out_hidden)
    return (
        out_grad.reshape((1,) + cotangent.shape),
        weight_grad[None, None],
        teacher_new[None, None],
        out_hidden.reshape((1,) + teacher_in.shape),
    )


vmem = pl.BlockSpec(memory_space=pltpu.VMEM)
smem = pl.BlockSpec(memory_space=pltpu.SMEM)
anywhere = pl.BlockSpec(memory_space=pl.ANY)
in_hbm = pl.BlockSpec(memory_space=pltpu.HBM)
params = pltpu.CompilerParams(vmem_limit_bytes=40 * 2**20)


def call(body, name, operands, spaces, out_shape, out_spaces, **more):
    return pl.pallas_call(
        body,
        in_specs=spaces,
        out_specs=out_spaces,
        out_shape=out_shape,
        compiler_params=params,
        name=name,
        **more,
    )(*operands)


def shaped(shape, dtype=bf16):
    return jax.ShapeDtypeStruct(shape, dtype)


def window(block, size):
    return pl.ds(pl.multiple_of(block * size, size), size)


class Plan:
    def __init__(self, sections):
        self.section, self.group, self.total, self.back = 0, 1, 2, 3
        self.ahead = self.back + sections + 1
        self.done_back = self.ahead + sections + 1
        self.done_ahead = self.done_back + sections
        self.size = self.done_ahead + sections


def plan_kernel(where, counts_ref, section_ref, group_ref, out_ref):
    sections = counts_ref.shape[0]
    out_ref[where.section] = section_ref[0]
    out_ref[where.group] = group_ref[0]
    seen = jnp.int32(0)
    for s in range(sections):
        out_ref[where.ahead + seen] = jnp.int32(s)
        seen = seen + (counts_ref[s] > 0).astype(jnp.int32)
        out_ref[where.done_ahead + s] = seen
    out_ref[where.total] = seen
    out_ref[where.ahead + sections] = jnp.int32(0)
    seen = jnp.int32(0)
    for s in reversed(range(sections)):
        out_ref[where.back + seen] = jnp.int32(s)
        seen = seen + (counts_ref[s] > 0).astype(jnp.int32)
        out_ref[where.done_back + s] = seen
    out_ref[where.back + sections] = jnp.int32(0)


def make_plan(where, counts):
    me = [lax.axis_index(axis).astype(jnp.int32)[None] for axis in ("section", "fsdp")]
    return call(
        functools.partial(plan_kernel, where),
        "make_plan",
        (counts, *me),
        [smem] * 3,
        shaped((where.size,), jnp.int32),
        smem,
    )


def first_kernel(where, plan, order, cot, pre, near_out, far_out, grad_out):
    sections, _, columns = near_out.shape[1:]
    me = plan[where.section]
    grad_out[...] = cot[order[me]]
    for distance in range(sections):
        target = me ^ distance
        out = (near_out, far_out)[distance & 1]
        for slot in range(sections):
            out[distance >> 1, pl.ds(slot ^ target, 1)] = times_slope(
                cot[order[slot], :, window(target, columns)],
                pre[slot, :, window(target, columns)],
            )[None]


def first_slopes(where, plan, order, cot, pre):
    sections, part, wide = pre.shape
    half = shaped((sections // 2, sections, part, wide // sections))
    return call(
        functools.partial(first_kernel, where),
        "first_slopes",
        (plan, order, cot, pre),
        [smem, smem, vmem, vmem],
        [half, half, shaped((part, wide))],
        [vmem] * 3,
    )


def weights_kernel(where, plan, student_ref, teacher_ref, new_ref, s_near, s_far, t_near, t_far):
    sections, columns = 2 * s_near.shape[0], s_near.shape[2]
    new_ref[...] = momentum * teacher_ref[...] + (1.0 - momentum) * student_ref[...].astype(f32)
    for distance in range(sections):
        cols = window(plan[where.section] ^ distance, columns)
        (s_near, s_far)[distance & 1][distance >> 1] = student_ref[:, cols]
        (t_near, t_far)[distance & 1][distance >> 1] = new_ref[:, cols].astype(bf16)


def split_weights(where, plan, student, teacher, sections):
    deep, wide = student.shape
    tile = 64
    columns = wide // sections
    whole = pl.BlockSpec((tile, wide), lambda i: (i, 0))
    half = pl.BlockSpec((sections // 2, tile, columns), lambda i: (0, i, 0))
    out = shaped((sections // 2, deep, columns))
    return call(
        functools.partial(weights_kernel, where),
        "split_weights",
        (plan, student, teacher),
        [smem, whole, whole],
        [shaped(teacher.shape, f32)] + [out] * 4,
        [whole] + [half] * 4,
        grid=(deep // tile,),
    )


def rows_kernel(where, plan, inputs_ref, pre_ref, near_out, far_out):
    part = inputs_ref.shape[1]
    for distance in range(inputs_ref.shape[0]):
        target = plan[where.section] ^ distance
        out = (near_out, far_out)[distance & 1]
        out[distance >> 1, :part] = inputs_ref[target]
        out[distance >> 1, part:] = pre_ref[target]


def split_rows(where, plan, inputs, pre):
    sections, part, wide = inputs.shape
    half = shaped((sections // 2, 2 * part, wide))
    return call(
        functools.partial(rows_kernel, where),
        "split_rows",
        (plan, inputs, pre),
        [smem, vmem, vmem],
        [half, half],
        [vmem] * 2,
    )


def send_kernel(where, root_at, plan, place, *refs):
    count = len(root_at)
    outs, sem = refs[2 * count : 3 * count], refs[3 * count]
    for i, at in enumerate(root_at):
        distance = plan[where.section] ^ plan[at + place[0]]
        for core in (0, 1):

            @pl.when((distance & 1) == core)
            def _(i=i, core=core):
                pltpu.make_async_copy(refs[2 * i + core].at[1], outs[i], sem.at[i]).start()

    for i in range(count):
        pltpu.make_async_copy(refs[2 * i].at[1], outs[i], sem.at[i]).wait()


def sends(where, plan, place, roots, pairs):
    flat = [half for pair in pairs for half in pair]
    return call(
        functools.partial(send_kernel, where, tuple(roots)),
        "send_blocks",
        (plan, place, *flat),
        [smem, smem] + [anywhere] * len(flat),
        [shaped(near.shape[1:]) for near, _ in pairs],
        [vmem] * len(pairs),
        scratch_shapes=[pltpu.SemaphoreType.DMA((len(pairs),))],
    )


def across(where, plan, place, roots, pairs):
    return [swap(block, "section", 2) for block in sends(where, plan, place, roots, pairs)]


def fetch(distance, near, far, came, held, sem):
    choices = ((near.at[0], 0), (far.at[0], 1), (came, 2), (came, 3))
    for source, at in choices:

        @pl.when(distance == at)
        def _(source=source):
            pltpu.make_async_copy(source, held, sem).start()

    pltpu.make_async_copy(came, held, sem).wait()


def take_kernel(where, plan, place, near, far, came, inputs_out, pre_out, sem):
    distance = plan[where.section] ^ plan[where.back + place[0]]
    part = inputs_out.shape[0]
    for j, out in enumerate((inputs_out, pre_out)):
        rows = pl.ds(j * part, part)
        for source, at in ((near.at[0], 0), (far.at[0], 1), (came, 2), (came, 3)):

            @pl.when(distance == at)
            def _(source=source, out=out, rows=rows, j=j):
                pltpu.make_async_copy(source.at[rows], out, sem.at[j]).start()

    for j, out in enumerate((inputs_out, pre_out)):
        pltpu.make_async_copy(came.at[pl.ds(j * part, part)], out, sem.at[j]).wait()


def take_rows(where, plan, place, near, far, came):
    part = came.shape[0] // 2
    return call(
        functools.partial(take_kernel, where),
        "take_rows",
        (plan, place, near, far, came),
        [smem, smem] + [anywhere] * 3,
        [shaped((part, came.shape[1]))] * 2,
        [vmem] * 2,
        scratch_shapes=[pltpu.SemaphoreType.DMA((2,))],
    )


def choose_kernel(where, plan, near, far, came, out, sem):
    distance = plan[where.section] ^ plan[where.back]
    fetch(distance, near, far, came, out, sem)


def choose(where, plan, near, far, came):
    return call(
        functools.partial(choose_kernel, where),
        "choose",
        (plan, near, far, came),
        [smem] + [anywhere] * 3,
        shaped(came.shape),
        vmem,
        scratch_shapes=[pltpu.SemaphoreType.DMA],
    )


def features_kernel(inputs_ref, hidden_ref, out_ref):
    groups, _, deep = out_ref.shape
    part = inputs_ref.shape[0]
    for rows, ref in ((pl.ds(0, part), inputs_ref), (pl.ds(part, hidden_ref.shape[0]), hidden_ref)):
        normed = normalize(ref[...])[0].astype(bf16)
        for j in range(groups):
            out_ref[j, rows] = normed[:, j * deep : (j + 1) * deep]


def features(inputs, hidden, groups):
    rows = inputs.shape[0] + hidden.shape[0]
    return call(
        features_kernel,
        "features",
        (inputs, hidden),
        [vmem, vmem],
        shaped((groups, rows, inputs.shape[1] // groups)),
        vmem,
    )


def back_kernel(where, plan, place, slopes_ref, near, far, came, stay_out, go_out, weight, sem):
    groups, sections, part, columns = slopes_ref.shape
    distance = plan[where.section] ^ plan[where.back + place[0]]
    fetch(distance, near, far, came, weight, sem)
    for k in range(groups):
        dn = lax.dot_general(
            slopes_ref[k].reshape(sections * part, columns),
            weight[...],
            (((1,), (1,)), ((), ())),
            preferred_element_type=f32,
        ).astype(bf16)
        dn = dn.reshape(sections, part, weight.shape[0])
        for s in range(sections):
            out = (stay_out, go_out)[s & 1]
            out[s >> 1, pl.ds(plan[where.group] ^ k, 1)] = dn[s][None]


def back_product(where, plan, place, slopes, near, far, came):
    groups, sections, part, _ = slopes.shape
    out = shaped((sections // 2, groups, part, came.shape[0]))
    return call(
        functools.partial(back_kernel, where),
        "back_product",
        (plan, place, slopes, near, far, came),
        [smem, smem, vmem] + [anywhere] * 3,
        [out, out],
        [vmem] * 2,
        scratch_shapes=[pltpu.VMEM(came.shape, bf16), pltpu.SemaphoreType.DMA],
    )


def ahead_kernel(where, part, plan, place, feats_ref, near, far, came, stay_out, go_out, weight, sem):
    sections, groups, rows, deep = feats_ref.shape
    part_f, columns = rows - part, came.shape[1]
    distance = plan[where.section] ^ plan[where.ahead + place[0]]
    fetch(distance, near, far, came, weight, sem)
    side = plan[where.group] & 1
    for s in range(sections):
        pre = jnp.dot(
            feats_ref[s, :, part:, :].reshape(groups * part_f, deep),
            weight[...],
            preferred_element_type=f32,
        ).astype(bf16)
        pre = pre.reshape(groups, part_f, columns)
        for j in range(0, groups, 2):
            seat = (plan[where.group] ^ j) >> 1
            stay_out[pl.ds(seat, 1), s] = jnp.where(side == 0, pre[j], pre[j + 1])[None]
            go_out[pl.ds(seat, 1), s] = jnp.where(side == 0, pre[j + 1], pre[j])[None]


def ahead_product(where, part, plan, place, feats, near, far, came):
    sections, groups, rows, _ = feats.shape
    out = shaped((groups // 2, sections, rows - part, came.shape[1]))
    return call(
        functools.partial(ahead_kernel, where, part),
        "ahead_product",
        (plan, place, feats, near, far, came),
        [smem, smem, vmem] + [anywhere] * 3,
        [out, out],
        [vmem] * 2,
        scratch_shapes=[pltpu.VMEM(came.shape, bf16), pltpu.SemaphoreType.DMA],
    )


def grad_kernel(where, scale, plan, feats_ref, slopes_ref, out_ref, total_ref):
    groups, sections, part, columns = slopes_ref.shape
    deep = feats_ref.shape[3]
    for k in range(groups):
        feats = feats_ref[:, pl.ds(plan[where.group] ^ k, 1), :part, :]
        term = lax.dot_general(
            feats.reshape(sections * part, deep),
            slopes_ref[k].reshape(sections * part, columns),
            (((0,), (0,)), ((), ())),
            preferred_element_type=f32,
        )
        if k == 0:
            total_ref[...] = term
        else:
            total_ref[...] += term
    out_ref[...] = (scale * total_ref[...]).astype(bf16)


def grad_product(where, scale, plan, feats, slopes):
    size = (feats.shape[3], slopes.shape[3])
    return call(
        functools.partial(grad_kernel, where, scale),
        "grad_product",
        (plan, feats, slopes),
        [smem, vmem, vmem],
        shaped(size),
        vmem,
        scratch_shapes=[pltpu.VMEM(size, f32)],
    )


def slopes_kernel(where, plan, grad_ref, pre_ref, out_ref):
    sections, _, columns = out_ref.shape
    for distance in range(sections):
        cols = window(plan[where.section] ^ distance, columns)
        out_ref[distance] = times_slope(grad_ref[:, cols], pre_ref[:, cols])


def slope_blocks(where, plan, grad, pre, sections):
    part, wide = pre.shape
    return call(
        functools.partial(slopes_kernel, where),
        "slope_blocks",
        (plan, grad, pre),
        [smem, vmem, vmem],
        shaped((sections, part, wide // sections)),
        vmem,
    )


def write_seen(done, sections, plan, place, values, outs, sem):
    for start in (True, False):
        for s in range(sections):

            @pl.when(plan[done + s] == place[0] + 1)
            def _(s=s, start=start):
                copy = pltpu.make_async_copy(values, outs.at[s], sem.at[s])
                copy.start() if start else copy.wait()


def update_kernel(where, plan, place, grad_ref, inputs_ref, dn_ref, old, out_ref, outs, sem):
    groups = dn_ref.shape[0]
    dn = jnp.concatenate([dn_ref[j].astype(f32) for j in range(groups)], axis=1)
    normed, factor = normalize(inputs_ref[...])
    grad = grad_ref[...].astype(f32) + factor * (
        dn - normed * jnp.mean(dn * normed, axis=-1, keepdims=True)
    )
    out_ref[...] = grad.astype(bf16)
    write_seen(where.done_back, old.shape[0], plan, place, out_ref, outs, sem)


def update(where, plan, place, grad, inputs, dn, outs):
    return call(
        functools.partial(update_kernel, where),
        "update",
        (plan, place, grad, inputs, dn, outs),
        [smem, smem, vmem, vmem, vmem, anywhere],
        [shaped(grad.shape), shaped(outs.shape)],
        [vmem, anywhere],
        scratch_shapes=[pltpu.SemaphoreType.DMA((outs.shape[0],))],
        input_output_aliases={5: 1},
    )


def hidden_kernel(where, plan, place, hidden_ref, pre_ref, old, out_ref, outs, sem):
    sections, _, columns = pre_ref.shape
    for distance in range(sections):
        cols = window(plan[where.section] ^ distance, columns)
        pre = pre_ref[distance].astype(f32)
        gelu = 0.5 * pre * (1.0 + lax.erf(pre / math.sqrt(2.0)))
        out_ref[:, cols] = (hidden_ref[:, cols].astype(f32) + gelu).astype(bf16)
    write_seen(where.done_ahead, old.shape[0], plan, place, out_ref, outs, sem)


def update_hidden(where, plan, place, hidden, pre, outs):
    return call(
        functools.partial(hidden_kernel, where),
        "update_hidden",
        (plan, place, hidden, pre, outs),
        [smem, smem, vmem, vmem, anywhere],
        [shaped(hidden.shape), shaped(outs.shape)],
        [vmem, anywhere],
        scratch_shapes=[pltpu.SemaphoreType.DMA((outs.shape[0],))],
        input_output_aliases={4: 1},
    )


def store_kernel(where, plan, place, *refs):
    terms, out, sem = refs[:4], refs[5], refs[6]
    columns = terms[0].shape[1]

    @pl.when(plan[where.section] == plan[where.back + place[0]])
    def _():
        copies = [
            pltpu.make_async_copy(
                term, out.at[:, window(plan[where.section] ^ distance, columns)], sem.at[distance]
            )
            for distance, term in enumerate(terms)
        ]
        for copy in copies:
            copy.start()
        for copy in copies:
            copy.wait()


def store(where, plan, place, terms, old):
    return call(
        functools.partial(store_kernel, where),
        "store",
        (plan, place, *terms, old),
        [smem, smem] + [anywhere] * 5,
        shaped(old.shape),
        anywhere,
        scratch_shapes=[pltpu.SemaphoreType.DMA((4,))],
        input_output_aliases={6: 0},
    )


def pack_kernel(where, plan, grads, hiddens, *refs):
    outs, sem = refs[:-1], refs[-1]
    part = grads.shape[1]
    for wait in (False, True):
        for distance, out in enumerate(outs):
            target = plan[where.section] ^ distance
            for j, (source, rows) in enumerate(
                ((grads, pl.ds(0, part)), (hiddens, pl.ds(part, hiddens.shape[1])))
            ):
                copy = pltpu.make_async_copy(source.at[target], out.at[rows], sem.at[2 * distance + j])
                copy.wait() if wait else copy.start()


def pack(where, plan, grads, hiddens):
    sections, part, width = grads.shape
    out = shaped((part + hiddens.shape[1], width))
    return call(
        functools.partial(pack_kernel, where),
        "pack",
        (plan, grads, hiddens),
        [smem, anywhere, anywhere],
        [out] * sections,
        [vmem] * sections,
        scratch_shapes=[pltpu.SemaphoreType.DMA((2 * sections,))],
    )


def unpack_kernel(where, plan, *refs):
    pieces, (grads, hiddens, sem) = refs[:-3], refs[-3:]
    part = grads.shape[1]
    for wait in (False, True):
        for distance, piece in enumerate(pieces):
            source = plan[where.section] ^ distance
            for j, (out, rows) in enumerate(
                ((grads, pl.ds(0, part)), (hiddens, pl.ds(part, hiddens.shape[1])))
            ):
                copy = pltpu.make_async_copy(piece.at[rows], out.at[source], sem.at[2 * distance + j])
                copy.wait() if wait else copy.start()


def unpack(where, plan, pieces, part):
    rows, width = pieces[0].shape
    return call(
        functools.partial(unpack_kernel, where),
        "unpack",
        (plan, *pieces),
        [smem] + [anywhere] * len(pieces),
        [shaped((len(pieces), part, width)), shaped((len(pieces), rows - part, width))],
        [in_hbm] * 2,
        scratch_shapes=[pltpu.SemaphoreType.DMA((2 * len(pieces),))],
    )


def from_sections(block):
    beside = swap(block, "section", 1)
    over = swap(block, "section", 2)
    return [block, beside, over, swap(over, "section", 1)]


def to_sections(blocks):
    return jnp.stack([blocks[0]] + [swap(blocks[k], "section", k) for k in (1, 2, 3)])


def from_groups(block):
    line = [block] + [swap(block, "fsdp", bits) for bits in (2, 4, 6)]
    other = [swap(b, "fsdp", 1) for b in line]
    return jnp.stack([b for pair in zip(line, other) for b in pair])


def sum_halves(stay, go, axis):
    near = add(stay, swap(go, axis, 1)).astype(bf16)
    total = near[0].astype(f32)
    for k in range(1, near.shape[0]):
        total = total + swap(near[k], axis, 2 * k).astype(f32)
    return total.astype(bf16)


def fence(*values):
    return lax.optimization_barrier(values)


def on_four_by_eight(
    student_w, teacher_w, saved_in, saved_pre, cotangent, slot_order, layer_counts, teacher_in
):
    sections = lax.axis_size("section")
    groups = lax.axis_size("fsdp")
    slots, tokens, width = cotangent.shape
    student = student_w[0, 0]
    deep, wide = student.shape
    rows = slots * tokens
    part = rows // sections
    part_f = teacher_in.shape[0] * tokens // sections
    scale = 1.0 / math.sqrt(rows * groups)
    where = Plan(sections)
    plan = make_plan(where, layer_counts)
    inputs_own = saved_in[0, 0].reshape(sections, part, width)
    pre_own = saved_pre[0, 0].reshape(sections, part, wide)

    def to_groups(blocks):
        return lax.all_to_all(blocks, "fsdp", 0, 0, tiled=True)

    def stage(place, grad, hidden, slopes, inputs, outs, spreads, first=False):
        weight, low, saved = spreads
        outs_grad, outs_hidden, weight_grad = outs
        if first:
            feats = to_groups(features(inputs, hidden, groups))
            feats, slopes = fence(feats, slopes)
            came = across(where, plan, place, (where.ahead, where.back), (low, weight))
            slopes = from_groups(slopes)
        else:
            came = across(where, plan, place, (where.ahead, where.back), (low, weight))
            line = [slopes] + [swap(slopes, "fsdp", bits) for bits in (2, 4, 6)]
            line[3], inputs, hidden = fence(line[3], inputs, hidden)
            feats = to_groups(features(inputs, hidden, groups))
            slopes = jnp.stack([b for near in line for b in (near, swap(near, "fsdp", 1))])
        low_came, weight_came = came
        feats = jnp.stack(from_sections(feats))
        pre = ahead_product(where, part, plan, place, feats, *low, low_came)
        pre = to_sections(sum_halves(*pre, "fsdp"))
        hidden, outs_hidden = update_hidden(where, plan, place, hidden, pre, outs_hidden)
        dn = back_product(where, plan, place, slopes, *weight, weight_came)
        dn = lax.all_to_all(sum_halves(*dn, "section"), "fsdp", 0, 0, tiled=True)
        grad, outs_grad = update(where, plan, place, grad, inputs, dn, outs_grad)
        terms = from_sections(grad_product(where, scale, plan, feats, slopes))
        weight_grad = store(where, plan, place, terms, weight_grad)
        (came,) = across(where, plan, place + 1, (where.back,), (saved,))
        inputs, pre = take_rows(where, plan, place + 1, *saved, came)
        return grad, hidden, inputs, pre, (outs_grad, outs_hidden, weight_grad)

    first = jnp.zeros((1,), jnp.int32)
    near, far, grad = first_slopes(where, plan, slot_order, cotangent, pre_own)
    far = swap(far, "section", 1)
    (came,) = across(where, plan, first, (where.back,), ((near, far),))
    slopes = choose(where, plan, near, far, came)
    hidden = lax.dynamic_slice(
        teacher_in.reshape(-1, width),
        (lax.axis_index("section") * part_f, 0),
        (part_f, width),
        allow_negative_indices=False,
    )
    near, far = split_rows(where, plan, inputs_own, pre_own)
    saved = (near, swap(far, "section", 1))
    (came,) = across(where, plan, first, (where.back,), (saved,))
    inputs, _ = take_rows(where, plan, first, *saved, came)
    teacher_new, s_near, s_far, t_near, t_far = split_weights(
        where, plan, student, teacher_w[0, 0], sections
    )
    spreads = ((s_near, swap(s_far, "section", 1)), (t_near, swap(t_far, "section", 1)), saved)
    outs = (
        jnp.broadcast_to(grad, (sections,) + grad.shape),
        jnp.broadcast_to(hidden, (sections,) + hidden.shape),
        jnp.zeros((deep, wide), bf16),
    )
    grad, hidden, inputs, pre, outs = stage(
        first, grad, hidden, slopes, inputs, outs, spreads, True
    )

    def next_stage(carry):
        place, grad, hidden, inputs, pre, outs = carry
        slopes = to_sections(slope_blocks(where, plan, grad, pre, sections))
        grad, hidden, inputs, pre, outs = stage(
            place[None], grad, hidden, slopes, inputs, outs, spreads
        )
        return place + 1, grad, hidden, inputs, pre, outs

    total = plan[where.total]
    carry = (jnp.int32(1), grad, hidden, inputs, pre, outs)
    outs = lax.while_loop(lambda c: c[0] < total, next_stage, carry)[-1]
    blocks = pack(where, plan, *outs[:2])
    pieces = [blocks[0]] + [swap(blocks[k], "section", k) for k in (1, 2, 3)]
    input_grad, teacher_out = unpack(where, plan, pieces, part)
    return (
        input_grad.reshape((1,) + cotangent.shape),
        outs[2][None, None],
        teacher_new[None, None],
        teacher_out.reshape((1,) + teacher_in.shape),
    )


def solution(mesh):
    in_specs = (
        P("section", None, "fsdp", None),
        P("section", None, "fsdp", None),
        P("section", None, None, "fsdp", None),
        P("section", None, None, "fsdp", None),
        P(None, "fsdp", None),
        P(),
        P(),
        P(None, "fsdp", None),
    )
    out_specs = (
        P("section", None, "fsdp", None),
        P("section", None, "fsdp", None),
        P("section", None, "fsdp", None),
        P("section", None, "fsdp", None),
    )
    sizes = dict(mesh.shape)
    fits = sizes["section"] == 4 and sizes["fsdp"] == 8
    return jax.shard_map(
        on_four_by_eight if fits else on_any_mesh, mesh=mesh, in_specs=in_specs, out_specs=out_specs, check_vma=False
    )
```
